256 devices in a mesh: wide: 32 (over z, x), narrow: 8 (over y, core).
Axes of the slice: x: 4, y: 4, z: 8, core: 2. Of those that a mesh axis runs over, the one named last changes fastest.
Arguments:
- activations: bfloat16 [131072, 8192], P(('wide', 'narrow')), may hold values from -64 to 64
- test_matrix: bfloat16 [8192, 320], replicated, may hold values from -0.0625 to 0.0625
Outputs:
- basis: float32 [131072, 320], P(('wide', 'narrow'))
- coeffs: float32 [320, 8192], P(None, 'narrow')
The draws below stay inside these ranges and needn't reach their ends.
All inputs are finite; a program needn't handle non-finite values.
Results may differ from the reference program's by a relative error of at most 0.00083.
Values sent between devices are 32-bit elements; how exact they have to be, the bound alone decides.
A program may use at most 128 MiB of HBM per device.

```python
import math
import jax
import jax.numpy as jnp
from jax import lax

D = 8192
K = 320
TOKENS = 131072


def draw_activations(key, part):
    key = jax.random.fold_in(key, 11)
    keys = jax.random.split(key, 4)
    rise = 3.0 ** (jnp.arange(TOKENS, dtype=jnp.float32) / (TOKENS - 1) - 0.5)
    col_scale = jnp.exp(jax.random.uniform(keys[3], (1, D), jnp.float32, math.log(0.3), math.log(3.0)))
    noise = jnp.clip(jax.random.normal(keys[0], (TOKENS, D), jnp.float32), -4.0, 4.0)
    row_scale = jnp.exp(jax.random.uniform(keys[2], (TOKENS, 1), jnp.float32, math.log(0.3), math.log(3.0)))
    return (noise * row_scale * rise[:, None] * col_scale).astype(jnp.bfloat16)


def scatter_about(stream_key, extent, scale, most, held_as=jnp.bfloat16):
    entries = jax.random.normal(stream_key, extent, jnp.float32) * scale
    return jnp.minimum(jnp.maximum(entries, -most), most).astype(held_as)


def setup_inputs(seed: int = 0) -> dict:
    key_of = jax.random.split(jax.random.key(seed), 3)
    return {
        "activations": draw_activations(jax.random.fold_in(key_of[2], 71), 0),
        "test_matrix": scatter_about(key_of[1], (D, K), D ** -0.5, 0.0625),
    }


def reference(activations, test_matrix):
    sketch = jnp.dot(activations.astype(jnp.float32), test_matrix.astype(jnp.float32), preferred_element_type=jnp.float32)
    gram = jnp.dot(sketch.T, sketch, precision=lax.Precision.HIGHEST)
    lower_factor = jnp.linalg.cholesky(gram)
    basis = lax.linalg.triangular_solve(lower_factor, sketch, left_side=False, lower=True, transpose_a=True) * math.sqrt(TOKENS)
    basis_half = basis.astype(jnp.bfloat16)
    projected = lax.dot_general(basis_half.astype(jnp.float32), activations.astype(jnp.float32), (((0,), (0,)), ((), ())), preferred_element_type=jnp.float32)
    coeffs = projected / TOKENS
    return (basis, coeffs)
```

```python
import functools
import math

import jax
import jax.numpy as jnp
from jax import lax
from jax.experimental import pallas as pl
from jax.experimental.pallas import tpu as pltpu
from jax.sharding import PartitionSpec as P

MESH = pl.DeviceIdType.MESH
HIGHEST = lax.Precision.HIGHEST
F32 = jnp.float32
BF16 = jnp.bfloat16
NX, NY, NZ = 4, 4, 8
BLOCK = 64
LANES = 128

CHUNKS = (("y", 0, 96), ("y", 96, 96), ("x", 192, 64), ("z", 256, 64))


def inverse_factor_block(block):
    n = block.shape[0]
    rows = lax.broadcasted_iota(jnp.int32, (n, n), 0)
    cols = lax.broadcasted_iota(jnp.int32, (n, n), 1)
    state = jnp.concatenate([block, jnp.where(rows == cols, 1.0, 0.0).astype(F32)], axis=1)
    row_in_group = lax.broadcasted_iota(jnp.int32, (8, 2 * n), 0)
    done = []
    for group in range(n // 8):
        left = n - 8 * group
        head = state[0:8, :]
        columns = [
            jnp.broadcast_to(state[:, 8 * group + j : 8 * group + j + 1], (left, 2 * n))
            for j in range(8)
        ]
        pivot_rows, pivot_cols = [], []
        for j in range(8):
            inv = lax.rsqrt(columns[j][j : j + 1, :])
            row = head[j : j + 1, :] * inv
            col = columns[j] * inv
            pivot_rows.append(row)
            pivot_cols.append(col)
            if j < 7:
                head = head - col[0:8] * row
            for later in range(j + 1, 8):
                columns[later] = columns[later] - col * col[later : later + 1, :]
        out = jnp.broadcast_to(pivot_rows[0], (8, 2 * n))
        for j in range(1, 8):
            out = jnp.where(row_in_group == j, pivot_rows[j], out)
        done.append(out)
        if left > 8:
            state = state[8:, :]
            for j in range(8):
                state = state - pivot_cols[j][8:] * pivot_rows[j]
    return jnp.concatenate(done, axis=0)[:, n:]


def factor_step(m_ref, step):
    k = m_ref.shape[0]
    lo, hi = step * BLOCK, (step + 1) * BLOCK
    inverse = inverse_factor_block(m_ref[lo:hi, lo:hi])
    rows = lax.broadcasted_iota(jnp.int32, (BLOCK, BLOCK), 0)
    cols = lax.broadcasted_iota(jnp.int32, (BLOCK, BLOCK), 1)
    m_ref[lo:hi, lo:hi] = jnp.where(rows == cols, 1.0, 0.0).astype(F32)
    panel = jnp.dot(inverse, m_ref[lo:hi, :], precision=HIGHEST, preferred_element_type=F32)
    m_ref[lo:hi, :] = panel
    if hi < k:
        m_ref[hi:, lo:hi] = jnp.zeros((k - hi, BLOCK), F32)
        m_ref[hi:, :] -= lax.dot_general(
            panel[:, hi:], panel, (((0,), (0,)), ((), ())),
            precision=HIGHEST, preferred_element_type=F32,
        )


def kernel(n_total, a_hbm, om_hbm, basis_ref, coef_ref,
           a_buf, om_buf, sketch, halves, to_core, from_core, part, total,
           folded, g_core, g_plane, g_line, g_sum, mat, load_sem, sems, *bufs):
    k = sketch.shape[1]
    wide, narrow = lax.axis_index("wide"), lax.axis_index("narrow")
    x, z = lax.rem(wide, NX), wide // NX
    y, c = narrow // 2, lax.rem(narrow, 2)

    def device(xx, yy, zz, cc):
        return (zz * NX + xx, yy * 2 + cc)

    sibling = device(x, y, z, 1 - c)
    on_x = [(lax.rem(x + d, NX), device(lax.rem(x + d, NX), y, z, c)) for d in range(1, NX)]
    on_y = [(lax.rem(y + d, NY), device(x, lax.rem(y + d, NY), z, c)) for d in range(1, NY)]
    on_z = [(lax.rem(z + d, NZ), device(x, y, lax.rem(z + d, NZ), c)) for d in range(1, NZ)]
    place = y * NX + x
    on_plane = []
    for d in range(1, NX * NY):
        other = lax.rem(place + d, NX * NY)
        on_plane.append((other, device(lax.rem(other, NX), other // NX, z, c)))

    used = [0]
    pending = []

    def exchange(size_like):
        at = used[0]
        used[0] += 2
        pending.append((at, size_like))
        return at

    def send(at, src, dst, to):
        pltpu.make_async_remote_copy(
            src_ref=src, dst_ref=dst, send_sem=sems.at[at], recv_sem=sems.at[at + 1],
            device_id=to, device_id_type=MESH,
        ).start()

    def wait_bytes(sem, like):
        pltpu.make_async_copy(like, like, sem).wait()

    def received(at, like):
        wait_bytes(sems.at[at + 1], like)

    barrier = pltpu.get_barrier_semaphore()
    partners = [sibling] + [to for _, to in on_plane] + [to for _, to in on_z]
    n_blocks, _, width = a_buf.shape
    loads = []
    for j in range(n_blocks):
        loads.append((
            pltpu.make_async_copy(a_hbm.at[:, pl.ds(j * width, width)], a_buf.at[j], load_sem.at[j]),
            pltpu.make_async_copy(om_hbm.at[pl.ds(j * width, width), :], om_buf.at[j], load_sem.at[n_blocks + j]),
        ))
    for first, second in loads:
        first.start()
        second.start()
    for to in partners:
        pl.semaphore_signal(barrier, inc=1, device_id=to, device_id_type=MESH)

    for j in range(n_blocks):
        loads[j][0].wait()
        loads[j][1].wait()
        term = jnp.dot(a_buf[j], om_buf[j], preferred_element_type=F32)
        if j == 0:
            sketch[...] = term
        else:
            sketch[...] += term

    gram = lax.dot_general(
        sketch[...], sketch[...], (((0,), (0,)), ((), ())),
        precision=HIGHEST, preferred_element_type=F32,
    )
    folded[...] = jnp.zeros(folded.shape, F32)
    folded[0:128, 0:k] = gram[0:128, :]
    folded[128:256, 0 : k - 128] = gram[128:256, 128:]
    folded[128 : k - 128, 256 : k] = gram[256:, 256:]

    pl.semaphore_wait(barrier, len(partners))
    half_rows = g_core.shape[0]
    mine = pl.multiple_of(c * half_rows, 8)
    yours = pl.multiple_of((1 - c) * half_rows, 8)
    ex_core = exchange(g_core)
    send(ex_core, folded.at[pl.ds(yours, half_rows)], g_core, sibling)

    value = sketch[...]
    high = value.astype(BF16)
    low = (value - high.astype(F32)).astype(BF16)
    halves[0:k, :] = high.T
    halves[k:, :] = low.T

    def project(block, dst, at):
        def columns(q, carry):
            cols = pl.ds(pl.multiple_of(q * 256, 256), 256)
            res = jnp.dot(halves[...], a_buf[block, :, cols], preferred_element_type=F32)
            res = res[0:k] + res[k:]
            dst[at, 2 * q] = res[:, 0:LANES]
            dst[at, 2 * q + 1] = res[:, LANES:]
            return carry

        lax.fori_loop(0, width // 256, columns, 0)

    owners = [lax.rem(y + d, NY) for d in (1, 2, 3, 0)]
    ex_owner = []
    for i, o in enumerate(owners):
        project(2 * o + 1 - c, to_core, o)
        at = exchange(from_core.at[o])
        ex_owner.append(at)
        send(at, to_core.at[o], from_core.at[o], sibling)
        project(2 * o + c, part, o)
        if i == 0:
            received(ex_core, g_core)
            folded[pl.ds(mine, half_rows)] += g_core[...]
            my_tile = pl.multiple_of(c * half_rows + place * 8, 8)
            ex_plane = exchange(g_plane)
            for d, (other, to) in enumerate(on_plane):
                src = folded.at[pl.ds(pl.multiple_of(c * half_rows + other * 8, 8), 8)]
                send(ex_plane, src, g_plane.at[d], to)

    class Chunk:
        pass

    chunks = []
    for i, (axis, first, n) in enumerate(CHUNKS):
        ch = Chunk()
        ch.axis, ch.first, ch.n, ch.q = axis, first, n, n // NX
        ch.b1, ch.b2, ch.b3 = bufs[3 * i : 3 * i + 3]
        ch.rows = pl.ds(first, n)
        ch.mine = pl.ds(pl.multiple_of(first + x * ch.q, 8), ch.q)
        ch.ex1 = exchange(ch.b1)
        chunks.append(ch)

    def quarter(ch, xx):
        return pl.ds(pl.multiple_of(ch.first + xx * ch.q, 8), ch.q)

    def first_sends(ch, i, o):
        if ch.axis == "y":
            if i < NY - 1:
                send(ch.ex1, part.at[o, :, ch.rows, :], ch.b1.at[i], on_y[i][1])
        elif ch.axis == "x":
            for d, (xx, to) in enumerate(on_x):
                send(ch.ex1, part.at[o, :, quarter(ch, xx), :], ch.b1.at[d, o], to)
        else:
            for d, (zz, to) in enumerate(on_z):
                send(ch.ex1, part.at[o, zz, ch.rows, :], ch.b1.at[d, o], to)

    def summed(buf, n):
        acc = buf[0]
        for d in range(1, n):
            acc = acc + buf[d]
        return acc

    def second(ch):
        received(ch.ex1, ch.b1)
        ch.ex2 = exchange(ch.b2)
        if ch.axis == "y":
            def add(t, carry):
                part[y, t, ch.rows, :] += ch.b1[0, t] + ch.b1[1, t] + ch.b1[2, t]
                return carry

            lax.fori_loop(0, NZ, add, 0)
            for d, (xx, to) in enumerate(on_x):
                send(ch.ex2, part.at[y, :, quarter(ch, xx), :], ch.b2.at[d], to)
        elif ch.axis == "x":
            def add(o, carry):
                part[o, :, ch.mine, :] += ch.b1[0, o] + ch.b1[1, o] + ch.b1[2, o]
                return carry

            lax.fori_loop(0, NY, add, 0)
            for d, (yy, to) in enumerate(on_y):
                send(ch.ex2, part.at[yy, :, ch.mine, :], ch.b2.at[d], to)
        else:
            def add(o, carry):
                acc = part[o, z, ch.rows, :]
                for d in range(NZ - 1):
                    acc = acc + ch.b1[d, o]
                part[o, z, ch.rows, :] = acc
                return carry

            lax.fori_loop(0, NY, add, 0)
            for d, (yy, to) in enumerate(on_y):
                send(ch.ex2, part.at[yy, z, ch.rows, :], ch.b2.at[d], to)

    def third(ch):
        received(ch.ex2, ch.b2)
        ch.ex3 = exchange(ch.b3)
        if ch.axis == "z":
            part[y, z, ch.rows, :] += summed(ch.b2, NY - 1)
            for d, (xx, to) in enumerate(on_x):
                send(ch.ex3, part.at[y, z, quarter(ch, xx), :], ch.b3.at[d], to)
        else:
            part[y, :, ch.mine, :] += summed(ch.b2, 3)
            for d, (zz, to) in enumerate(on_z):
                send(ch.ex3, part.at[y, zz, ch.mine, :], ch.b3.at[d], to)

    def fourth(ch):
        received(ch.ex3, ch.b3)
        total[z, ch.mine, :] = part[y, z, ch.mine, :] + summed(ch.b3, ch.b3.shape[0])
        ch.ex4 = exchange(total.at[pl.ds(0, NZ - 1), pl.ds(0, ch.q), :])
        for _, to in on_z:
            send(ch.ex4, total.at[z, ch.mine, :], total.at[z, ch.mine, :], to)

    def fifth(ch):
        received(ch.ex4, total.at[pl.ds(0, NZ - 1), pl.ds(0, ch.q), :])
        ch.ex5 = exchange(total.at[:, pl.ds(0, 3 * ch.q), :])
        for _, to in on_x:
            send(ch.ex5, total.at[:, ch.mine, :], total.at[:, ch.mine, :], to)

    def last(ch):
        received(ch.ex5, total.at[:, pl.ds(0, 3 * ch.q), :])

    def owner_ready(i):
        o = owners[i]
        received(ex_owner[i], from_core.at[o])

        def add(t, carry):
            part[o, t] += from_core[o, t]
            return carry

        lax.fori_loop(0, NZ, add, 0)
        for ch in chunks:
            first_sends(ch, i, o)

    tile = pl.ds(my_tile, 8)

    def gram_line():
        received(ex_plane, g_plane)
        g_line[z] = folded[tile, :] + summed(g_plane, NX * NY - 1)
        at = exchange(g_plane.at[pl.ds(0, NZ - 1)])
        for _, to in on_z:
            send(at, g_line.at[z], g_line.at[z], to)
        return at

    def gram_spread(at):
        received(at, g_plane.at[pl.ds(0, NZ - 1)])
        g_sum[tile, :] = summed(g_line, NZ)
        at = exchange(g_plane)
        for _, to in on_plane:
            send(at, g_sum.at[tile], g_sum.at[tile], to)
        return at

    def gram_core(at):
        received(at, g_plane)
        at = exchange(g_core)
        my_half = pl.ds(mine, half_rows)
        send(at, g_sum.at[my_half], g_sum.at[my_half], sibling)
        return at

    def gram_ready(at):
        received(at, g_core)
        mat[0:128, :] = g_sum[0:128, 0:k]
        mat[128:256, 128:] = g_sum[128:256, 0 : k - 128]
        mat[256:, 256:] = g_sum[128 : k - 128, 256 : k]

    y0, y1, xc, zc = chunks
    owner_ready(0)
    owner_ready(1)
    at = gram_line()
    owner_ready(2)
    owner_ready(3)
    at = gram_spread(at)
    at = gram_core(at)
    second(xc)
    gram_ready(at)
    factor_step(mat, 0)
    third(xc)
    second(y0)
    factor_step(mat, 1)
    fourth(xc)
    third(y0)
    factor_step(mat, 2)
    fifth(xc)
    second(zc)
    factor_step(mat, 3)
    fourth(y0)
    third(zc)
    factor_step(mat, 4)
    rows = lax.broadcasted_iota(jnp.int32, (k, k), 0)
    cols = lax.broadcasted_iota(jnp.int32, (k, k), 1)
    mat[...] = jnp.where(rows >= cols, mat[...], 0.0)
    second(y1)
    fifth(y0)
    fourth(zc)
    basis_ref[...] = lax.dot_general(
        sketch[...], mat[...], (((1,), (1,)), ((), ())),
        precision=HIGHEST, preferred_element_type=F32,
    ) * math.sqrt(n_total)
    third(y1)
    fifth(zc)
    fourth(y1)
    fifth(y1)
    for ch in chunks:
        last(ch)

    def finish(q, carry):
        cols = pl.ds(pl.multiple_of(q * 256, 256), 256)
        both = jnp.concatenate([total[2 * q], total[2 * q + 1]], axis=1)
        coef_ref[:, cols] = jnp.dot(
            mat[...], both, precision=HIGHEST, preferred_element_type=F32
        ) * (1.0 / math.sqrt(n_total))
        return carry

    lax.fori_loop(0, coef_ref.shape[1] // 256, finish, 0)
    for at, like in pending:
        wait_bytes(sems.at[at], like)


def per_device(activations, test_matrix):
    rows, d = activations.shape
    k = test_matrix.shape[1]
    n_total = rows * lax.axis_size("wide") * lax.axis_size("narrow")
    width = d // (2 * NY)
    bufs = []
    for axis, _, n in CHUNKS:
        q = n // NX
        if axis == "y":
            shapes = ((3, NZ, n, LANES), (3, NZ, q, LANES), (7, q, LANES))
        elif axis == "x":
            shapes = ((3, NY, NZ, q, LANES), (3, NZ, q, LANES), (7, q, LANES))
        else:
            shapes = ((7, NY, n, LANES), (3, n, LANES), (3, q, LANES))
        bufs += [pltpu.VMEM(s, F32) for s in shapes]
    block = (NY, NZ, k, LANES)
    return pl.pallas_call(
        functools.partial(kernel, n_total),
        out_shape=(
            jax.ShapeDtypeStruct((rows, k), F32),
            jax.ShapeDtypeStruct((k, width), F32),
        ),
        in_specs=[pl.BlockSpec(memory_space=pl.ANY)] * 2,
        out_specs=(pl.BlockSpec(memory_space=pltpu.VMEM), pl.BlockSpec(memory_space=pltpu.VMEM)),
        scratch_shapes=[
            pltpu.VMEM((d // width, rows, width), BF16),
            pltpu.VMEM((d // width, width, k), BF16),
            pltpu.VMEM((rows, k), F32),
            pltpu.VMEM((2 * k, rows), BF16),
            pltpu.VMEM(block, F32),
            pltpu.VMEM(block, F32),
            pltpu.VMEM(block, F32),
            pltpu.VMEM((NZ, k, LANES), F32),
            pltpu.VMEM((256, 384), F32),
            pltpu.VMEM((128, 384), F32),
            pltpu.VMEM((NX * NY - 1, 8, 384), F32),
            pltpu.VMEM((NZ, 8, 384), F32),
            pltpu.VMEM((256, 384), F32),
            pltpu.VMEM((k, k), F32),
            pltpu.SemaphoreType.DMA((2 * d // width,)),
            pltpu.SemaphoreType.DMA((64,)),
        ] + bufs,
        compiler_params=pltpu.CompilerParams(
            collective_id=0, has_side_effects=True, vmem_limit_bytes=56 * 1024 * 1024
        ),
        name="range_finder",
    )(activations, test_matrix)


def solution(mesh):
    return jax.shard_map(
        per_device,
        mesh=mesh,
        in_specs=(P(("wide", "narrow"), None), P()),
        out_specs=(P(("wide", "narrow"), None), P(None, "narrow")),
        check_vma=False,
    )
```

```python
import functools
import math

import jax
import jax.numpy as jnp
from jax import lax
from jax.experimental import pallas as pl
from jax.experimental.pallas import tpu as pltpu
from jax.sharding import PartitionSpec as P

MESH = pl.DeviceIdType.MESH
HIGHEST = lax.Precision.HIGHEST
F32 = jnp.float32
BF16 = jnp.bfloat16
NX, NY, NZ = 4, 4, 8
BLOCK = 64
LANES = 128

CHUNKS = (("y", 0, 96), ("y", 96, 96), ("x", 192, 64), ("z", 256, 64))


def inverse_factor_block(block):
    n = block.shape[0]
    rows = lax.broadcasted_iota(jnp.int32, (n, n), 0)
    cols = lax.broadcasted_iota(jnp.int32, (n, n), 1)
    state = jnp.concatenate([block, jnp.where(rows == cols, 1.0, 0.0).astype(F32)], axis=1)
    row_in_group = lax.broadcasted_iota(jnp.int32, (8, 2 * n), 0)
    done = []
    for group in range(n // 8):
        left = n - 8 * group
        head = state[0:8, :]
        columns = [
            jnp.broadcast_to(state[:, 8 * group + j : 8 * group + j + 1], (left, 2 * n))
            for j in range(8)
        ]
        pivot_rows, pivot_cols = [], []
        for j in range(8):
            inv = lax.rsqrt(columns[j][j : j + 1, :])
            row = head[j : j + 1, :] * inv
            col = columns[j] * inv
            pivot_rows.append(row)
            pivot_cols.append(col)
            if j < 7:
                head = head - col[0:8] * row
            for later in range(j + 1, 8):
                columns[later] = columns[later] - col * col[later : later + 1, :]
        out = jnp.broadcast_to(pivot_rows[0], (8, 2 * n))
        for j in range(1, 8):
            out = jnp.where(row_in_group == j, pivot_rows[j], out)
        done.append(out)
        if left > 8:
            state = state[8:, :]
            for j in range(8):
                state = state - pivot_cols[j][8:] * pivot_rows[j]
    return jnp.concatenate(done, axis=0)[:, n:]


def factor_step(m_ref, step):
    k = m_ref.shape[0]
    lo, hi = step * BLOCK, (step + 1) * BLOCK
    inverse = inverse_factor_block(m_ref[lo:hi, lo:hi])
    rows = lax.broadcasted_iota(jnp.int32, (BLOCK, BLOCK), 0)
    cols = lax.broadcasted_iota(jnp.int32, (BLOCK, BLOCK), 1)
    m_ref[lo:hi, lo:hi] = jnp.where(rows == cols, 1.0, 0.0).astype(F32)
    panel = jnp.dot(inverse, m_ref[lo:hi, :], precision=HIGHEST, preferred_element_type=F32)
    m_ref[lo:hi, :] = panel
    if hi < k:
        m_ref[hi:, lo:hi] = jnp.zeros((k - hi, BLOCK), F32)
        m_ref[hi:, :] -= lax.dot_general(
            panel[:, hi:], panel, (((0,), (0,)), ((), ())),
            precision=HIGHEST, preferred_element_type=F32,
        )


def kernel(n_total, a_hbm, om_hbm, basis_hbm, total_hbm, inv_hbm,
           a_buf, om_buf, sketch, halves, to_core, from_core, part, total,
           folded, g_core, g_plane, g_line, g_sum, mat, basis_t, load_sem, out_sem, sems, *bufs):
    rows_here, k = sketch.shape
    wide, narrow = lax.axis_index("wide"), lax.axis_index("narrow")
    x, z = lax.rem(wide, NX), wide // NX
    y, c = narrow // 2, lax.rem(narrow, 2)

    def device(xx, yy, zz, cc):
        return (zz * NX + xx, yy * 2 + cc)

    sibling = device(x, y, z, 1 - c)
    on_x = [(lax.rem(x + d, NX), device(lax.rem(x + d, NX), y, z, c)) for d in range(1, NX)]
    on_y = [(lax.rem(y + d, NY), device(x, lax.rem(y + d, NY), z, c)) for d in range(1, NY)]
    on_z = [(lax.rem(z + d, NZ), device(x, y, lax.rem(z + d, NZ), c)) for d in range(1, NZ)]
    place = y * NX + x
    on_plane = []
    for d in range(1, NX * NY):
        other = lax.rem(place + d, NX * NY)
        on_plane.append((other, device(lax.rem(other, NX), other // NX, z, c)))

    used = [0]
    pending = []

    def exchange(size_like):
        at = used[0]
        used[0] += 2
        pending.append((at, size_like))
        return at

    def send(at, src, dst, to):
        pltpu.make_async_remote_copy(
            src_ref=src, dst_ref=dst, send_sem=sems.at[at], recv_sem=sems.at[at + 1],
            device_id=to, device_id_type=MESH,
        ).start()

    def wait_bytes(sem, like):
        pltpu.make_async_copy(like, like, sem).wait()

    def received(at, like):
        wait_bytes(sems.at[at + 1], like)

    barrier = pltpu.get_barrier_semaphore()
    partners = [sibling] + [to for _, to in on_plane] + [to for _, to in on_z]
    n_blocks, _, width = a_buf.shape
    loads = []
    for j in range(n_blocks):
        loads.append((
            pltpu.make_async_copy(a_hbm.at[:, pl.ds(j * width, width)], a_buf.at[j], load_sem.at[j]),
            pltpu.make_async_copy(om_hbm.at[:, pl.ds(j * width, width)], om_buf.at[j], load_sem.at[n_blocks + j]),
        ))
    for first, second in loads:
        first.start()
        second.start()
    for to in partners:
        pl.semaphore_signal(barrier, inc=1, device_id=to, device_id_type=MESH)

    for j in range(n_blocks):
        loads[j][0].wait()
        loads[j][1].wait()
        term = lax.dot_general(
            a_buf[j], om_buf[j], (((1,), (1,)), ((), ())), preferred_element_type=F32
        )
        if j == 0:
            sketch[...] = term
        else:
            sketch[...] += term

    gram = lax.dot_general(
        sketch[...], sketch[...], (((0,), (0,)), ((), ())),
        precision=HIGHEST, preferred_element_type=F32,
    )
    folded[...] = jnp.zeros(folded.shape, F32)
    folded[0:128, 0:k] = gram[0:128, :]
    folded[128:256, 0 : k - 128] = gram[128:256, 128:]
    folded[128 : k - 128, 256 : k] = gram[256:, 256:]

    pl.semaphore_wait(barrier, len(partners))
    half_rows = g_core.shape[0]
    mine = pl.multiple_of(c * half_rows, 8)
    yours = pl.multiple_of((1 - c) * half_rows, 8)
    ex_core = exchange(g_core)
    send(ex_core, folded.at[pl.ds(yours, half_rows)], g_core, sibling)

    value = sketch[...]
    high = value.astype(BF16)
    low = (value - high.astype(F32)).astype(BF16)
    halves[:, 0:rows_here] = high.T
    halves[:, rows_here:] = low.T

    def project(block, dst, at):
        cols = a_buf[block]
        res = jnp.dot(
            halves[...], jnp.concatenate([cols, cols], axis=0), preferred_element_type=F32
        )
        for t in range(NZ):
            dst[at, t] = res[:, t * LANES : (t + 1) * LANES]

    owners = [lax.rem(y + d, NY) for d in (1, 2, 3, 0)]
    ex_owner = []
    for o in owners:
        project(2 * o + 1 - c, to_core, o)
        at = exchange(from_core.at[o])
        ex_owner.append(at)
        send(at, to_core.at[o], from_core.at[o], sibling)
    received(ex_core, g_core)
    folded[pl.ds(mine, half_rows)] += g_core[...]
    my_tile = pl.multiple_of(c * half_rows + place * 8, 8)
    ex_plane = exchange(g_plane)
    for d, (other, to) in enumerate(on_plane):
        src = folded.at[pl.ds(pl.multiple_of(c * half_rows + other * 8, 8), 8)]
        send(ex_plane, src, g_plane.at[d], to)

    class Chunk:
        pass

    chunks = []
    for i, (axis, first, n) in enumerate(CHUNKS):
        ch = Chunk()
        ch.axis, ch.first, ch.n, ch.q = axis, first, n, n // NX
        ch.b1, ch.b2, ch.b3 = bufs[3 * i : 3 * i + 3]
        ch.rows = pl.ds(first, n)
        ch.mine = pl.ds(pl.multiple_of(first + x * ch.q, 8), ch.q)
        ch.ex1 = exchange(ch.b1)
        chunks.append(ch)

    def quarter(ch, xx):
        return pl.ds(pl.multiple_of(ch.first + xx * ch.q, 8), ch.q)

    def first_sends(ch, i, o):
        if ch.axis == "y":
            if i < NY - 1:
                send(ch.ex1, part.at[o, :, ch.rows, :], ch.b1.at[i], on_y[i][1])
        elif ch.axis == "x":
            for d, (xx, to) in enumerate(on_x):
                send(ch.ex1, part.at[o, :, quarter(ch, xx), :], ch.b1.at[d, o], to)
        else:
            for d, (zz, to) in enumerate(on_z):
                send(ch.ex1, part.at[o, zz, ch.rows, :], ch.b1.at[d, o], to)

    def summed(buf, n):
        acc = buf[0]
        for d in range(1, n):
            acc = acc + buf[d]
        return acc

    def second(ch):
        received(ch.ex1, ch.b1)
        ch.ex2 = exchange(ch.b2)
        if ch.axis == "y":
            def add(t, carry):
                part[y, t, ch.rows, :] += ch.b1[0, t] + ch.b1[1, t] + ch.b1[2, t]
                return carry

            lax.fori_loop(0, NZ, add, 0)
            for d, (xx, to) in enumerate(on_x):
                send(ch.ex2, part.at[y, :, quarter(ch, xx), :], ch.b2.at[d], to)
        elif ch.axis == "x":
            def add(o, carry):
                part[o, :, ch.mine, :] += ch.b1[0, o] + ch.b1[1, o] + ch.b1[2, o]
                return carry

            lax.fori_loop(0, NY, add, 0)
            for d, (yy, to) in enumerate(on_y):
                send(ch.ex2, part.at[yy, :, ch.mine, :], ch.b2.at[d], to)
        else:
            def add(o, carry):
                acc = part[o, z, ch.rows, :]
                for d in range(NZ - 1):
                    acc = acc + ch.b1[d, o]
                part[o, z, ch.rows, :] = acc
                return carry

            lax.fori_loop(0, NY, add, 0)
            for d, (yy, to) in enumerate(on_y):
                send(ch.ex2, part.at[yy, z, ch.rows, :], ch.b2.at[d], to)

    def third(ch):
        received(ch.ex2, ch.b2)
        ch.ex3 = exchange(ch.b3)
        if ch.axis == "z":
            part[y, z, ch.rows, :] += summed(ch.b2, NY - 1)
            for d, (xx, to) in enumerate(on_x):
                send(ch.ex3, part.at[y, z, quarter(ch, xx), :], ch.b3.at[d], to)
        else:
            part[y, :, ch.mine, :] += summed(ch.b2, 3)
            for d, (zz, to) in enumerate(on_z):
                send(ch.ex3, part.at[y, zz, ch.mine, :], ch.b3.at[d], to)

    def fourth(ch):
        received(ch.ex3, ch.b3)
        total[z, ch.mine, :] = part[y, z, ch.mine, :] + summed(ch.b3, ch.b3.shape[0])
        ch.ex4 = exchange(total.at[pl.ds(0, NZ - 1), pl.ds(0, ch.q), :])
        for _, to in on_z:
            send(ch.ex4, total.at[z, ch.mine, :], total.at[z, ch.mine, :], to)

    def fifth(ch):
        received(ch.ex4, total.at[pl.ds(0, NZ - 1), pl.ds(0, ch.q), :])
        ch.ex5 = exchange(total.at[:, pl.ds(0, 3 * ch.q), :])
        for _, to in on_x:
            send(ch.ex5, total.at[:, ch.mine, :], total.at[:, ch.mine, :], to)

    def last(ch):
        received(ch.ex5, total.at[:, pl.ds(0, 3 * ch.q), :])

    def owner_ready(i):
        o = owners[i]
        project(2 * o + c, part, o)
        received(ex_owner[i], from_core.at[o])

        def add(t, carry):
            part[o, t] += from_core[o, t]
            return carry

        lax.fori_loop(0, NZ, add, 0)
        for ch in chunks:
            first_sends(ch, i, o)

    tile = pl.ds(my_tile, 8)

    def gram_line():
        received(ex_plane, g_plane)
        g_line[z] = folded[tile, :] + summed(g_plane, NX * NY - 1)
        at = exchange(g_plane.at[pl.ds(0, NZ - 1)])
        for _, to in on_z:
            send(at, g_line.at[z], g_line.at[z], to)
        return at

    def gram_spread(at):
        received(at, g_plane.at[pl.ds(0, NZ - 1)])
        g_sum[tile, :] = summed(g_line, NZ)
        at = exchange(g_plane)
        for _, to in on_plane:
            send(at, g_sum.at[tile], g_sum.at[tile], to)
        return at

    def gram_core(at):
        received(at, g_plane)
        at = exchange(g_core)
        my_half = pl.ds(mine, half_rows)
        send(at, g_sum.at[my_half], g_sum.at[my_half], sibling)
        return at

    def gram_ready(at):
        received(at, g_core)
        mat[0:128, :] = g_sum[0:128, 0:k]
        mat[128:256, 128:] = g_sum[128:256, 0 : k - 128]
        mat[256:, 256:] = g_sum[128 : k - 128, 256 : k]

    y0, y1, xc, zc = chunks
    owner_ready(0)
    owner_ready(1)
    at = gram_line()
    owner_ready(2)
    owner_ready(3)
    at = gram_spread(at)
    at = gram_core(at)
    second(xc)
    gram_ready(at)
    factor_step(mat, 0)
    third(xc)
    second(y0)
    factor_step(mat, 1)
    fourth(xc)
    third(y0)
    factor_step(mat, 2)
    fifth(xc)
    second(zc)
    factor_step(mat, 3)
    fourth(y0)
    third(zc)
    factor_step(mat, 4)
    rows = lax.broadcasted_iota(jnp.int32, (k, k), 0)
    cols = lax.broadcasted_iota(jnp.int32, (k, k), 1)
    mat[...] = jnp.where(rows >= cols, mat[...], 0.0)
    second(y1)
    fifth(y0)
    fourth(zc)
    basis_t[...] = lax.dot_general(
        mat[...], sketch[...], (((1,), (1,)), ((), ())),
        precision=HIGHEST, preferred_element_type=F32,
    ) * math.sqrt(n_total)
    outs = [
        pltpu.make_async_copy(mat, inv_hbm, out_sem.at[0]),
        pltpu.make_async_copy(basis_t, basis_hbm, out_sem.at[1]),
    ]
    for copy in outs:
        copy.start()
    third(y1)
    fifth(zc)
    fourth(y1)
    fifth(y1)
    for i, ch in enumerate(chunks):
        last(ch)
        copy = pltpu.make_async_copy(
            total.at[:, ch.rows, :], total_hbm.at[:, ch.rows, :], out_sem.at[2 + i]
        )
        copy.start()
        outs.append(copy)
    for copy in outs:
        copy.wait()
    for at, like in pending:
        wait_bytes(sems.at[at], like)


def finish_kernel(n_total, steps, basis_hbm, total_ref, inv_ref, basis_out, coef_ref, sem):
    copy = pltpu.make_async_copy(basis_hbm, basis_out, sem)

    @pl.when(pl.program_id(0) == 0)
    def _():
        copy.start()

    both = jnp.concatenate([total_ref[0], total_ref[1]], axis=1)
    coef_ref[...] = jnp.dot(
        inv_ref[...], both, precision=HIGHEST, preferred_element_type=F32
    ) * (1.0 / math.sqrt(n_total))

    @pl.when(pl.program_id(0) == steps - 1)
    def _():
        copy.wait()


def per_device(activations, test_matrix):
    rows, d = activations.shape
    k = test_matrix.shape[1]
    n_total = rows * lax.axis_size("wide") * lax.axis_size("narrow")
    width = d // (2 * NY)
    bufs = []
    for axis, _, n in CHUNKS:
        q = n // NX
        if axis == "y":
            shapes = ((3, NZ, n, LANES), (3, NZ, q, LANES), (7, q, LANES))
        elif axis == "x":
            shapes = ((3, NY, NZ, q, LANES), (3, NZ, q, LANES), (7, q, LANES))
        else:
            shapes = ((7, NY, n, LANES), (3, n, LANES), (3, q, LANES))
        bufs += [pltpu.VMEM(s, F32) for s in shapes]
    block = (NY, NZ, k, LANES)
    hbm = pl.BlockSpec(memory_space=pl.ANY)
    basis_t, total, inverse = pl.pallas_call(
        functools.partial(kernel, n_total),
        out_shape=(
            jax.ShapeDtypeStruct((k, rows), F32),
            jax.ShapeDtypeStruct((NZ, k, LANES), F32),
            jax.ShapeDtypeStruct((k, k), F32),
        ),
        in_specs=[hbm] * 2,
        out_specs=(hbm, hbm, hbm),
        scratch_shapes=[
            pltpu.VMEM((d // width, rows, width), BF16),
            pltpu.VMEM((d // width, k, width), BF16),
            pltpu.VMEM((rows, k), F32),
            pltpu.VMEM((k, 2 * rows), BF16),
            pltpu.VMEM(block, F32),
            pltpu.VMEM(block, F32),
            pltpu.VMEM(block, F32),
            pltpu.VMEM((NZ, k, LANES), F32),
            pltpu.VMEM((256, 384), F32),
            pltpu.VMEM((128, 384), F32),
            pltpu.VMEM((NX * NY - 1, 8, 384), F32),
            pltpu.VMEM((NZ, 8, 384), F32),
            pltpu.VMEM((256, 384), F32),
            pltpu.VMEM((k, k), F32),
            pltpu.VMEM((k, rows), F32),
            pltpu.SemaphoreType.DMA((2 * d // width,)),
            pltpu.SemaphoreType.DMA((2 + len(CHUNKS),)),
            pltpu.SemaphoreType.DMA((64,)),
        ] + bufs,
        compiler_params=pltpu.CompilerParams(
            collective_id=0, has_side_effects=True, vmem_limit_bytes=56 * 1024 * 1024
        ),
        name="range_finder",
    )(activations, test_matrix.T)
    steps = NZ // 2
    basis_t, coeffs = pl.pallas_call(
        functools.partial(finish_kernel, n_total, steps),
        grid=(steps,),
        out_shape=(
            jax.ShapeDtypeStruct((k, rows), F32),
            jax.ShapeDtypeStruct((k, width), F32),
        ),
        in_specs=[
            hbm,
            pl.BlockSpec((2, k, LANES), lambda i: (i, 0, 0)),
            pl.BlockSpec((k, k), lambda i: (0, 0)),
        ],
        out_specs=(hbm, pl.BlockSpec((k, 2 * LANES), lambda i: (0, i))),
        scratch_shapes=[pltpu.SemaphoreType.DMA],
        name="apply_inverse",
    )(basis_t, total, inverse)
    return basis_t.T, coeffs


def solution(mesh):
    return jax.shard_map(
        per_device,
        mesh=mesh,
        in_specs=(P(("wide", "narrow"), None), P()),
        out_specs=(P(("wide", "narrow"), None), P(None, "narrow")),
        check_vma=False,
    )
```

```python
import functools
import math

import jax
import jax.numpy as jnp
from jax import lax
from jax.experimental import pallas as pl
from jax.experimental.pallas import tpu as pltpu
from jax.sharding import PartitionSpec as P

MESH = pl.DeviceIdType.MESH
HIGHEST = lax.Precision.HIGHEST
F32 = jnp.float32
BF16 = jnp.bfloat16
NX, NY, NZ = 4, 4, 8
BLOCK = 64
LANES = 128
SEMAPHORES = 200

CHUNKS = (
    ("y", 0, 32, False),
    ("y", 32, 32, False),
    ("y", 64, 32, False),
    ("y", 96, 32, True),
    ("y", 128, 32, False),
    ("x", 160, 32, False),
    ("x", 192, 32, False),
    ("x", 224, 32, False),
    ("x", 256, 32, True),
    ("z", 288, 32, False),
)

ORDER = (
    ("owner", -1, 0), ("ya", 0, 0), ("ya", 1, 0), ("ya", 2, 0), ("ya", 3, 0), ("ya", 4, 0), ("xa", 5, 0),
    ("xa", 6, 0), ("xa", 7, 0), ("xa", 8, 0), ("za", 9, 0), ("gram_line", -1, 0), ("owner", -1, 1), ("xa", 5, 1),
    ("xa", 6, 1), ("xa", 7, 1), ("xa", 8, 1), ("za", 9, 1), ("xb", 5, 0), ("xb", 6, 0), ("owner", -1, 2),
    ("xa", 5, 2), ("xa", 6, 2), ("xa", 7, 2), ("xa", 8, 2), ("za", 9, 2), ("yb", 0, 0), ("xb", 7, 0), ("xb", 8, 0),
    ("yb", 1, 0), ("xb", 5, 1), ("xb", 6, 1), ("owner", -1, 3), ("xa", 5, 3), ("xa", 6, 3), ("xa", 7, 3),
    ("xa", 8, 3), ("za", 9, 3), ("yb", 2, 0), ("xb", 7, 1), ("xb", 8, 1), ("yb", 3, 0), ("xb", 5, 2), ("xb", 6, 2),
    ("xb", 7, 2), ("gram_spread", -1, 0), ("yb", 4, 0), ("xb", 8, 2), ("y2", 0, 0), ("xb", 5, 3), ("xb", 6, 3),
    ("xb", 7, 3), ("xb", 8, 3), ("y2", 1, 0), ("z2", 9, 0), ("y2", 2, 0), ("y3", 0, 0), ("y2", 3, 0), ("x2", 5, 0),
    ("gram_core", -1, 0), ("x2", 6, 0), ("x2", 7, 0), ("x2", 8, 0), ("gram_ready", -1, 0), ("factor", -1, 0),
    ("y3", 1, 0), ("z3", 9, 0), ("y3", 2, 0), ("c4", 0, 0), ("y2", 4, 0), ("x3", 5, 0), ("factor", -1, 1),
    ("y3", 3, 0), ("x3", 6, 0), ("factor", -1, 2), ("c4", 9, 0), ("c4", 1, 0), ("y3", 4, 0), ("x3", 7, 0),
    ("x3", 8, 0), ("c4", 2, 0), ("factor", -1, 3), ("c5", 0, 0), ("c4", 3, 0), ("c4", 5, 0), ("factor", -1, 4),
    ("c5", 9, 0), ("c4", 6, 0), ("basis", -1, 0), ("c5", 1, 0), ("c4", 4, 0), ("c4", 7, 0), ("c6", 0, 0),
    ("c5", 3, 0), ("c4", 8, 0), ("c5", 2, 0), ("c5", 5, 0), ("c6", 9, 0), ("c5", 6, 0), ("c6", 1, 0), ("c5", 8, 0),
    ("c5", 4, 0), ("c5", 7, 0), ("c6", 2, 0), ("c6", 5, 0), ("c6", 3, 0), ("c6", 6, 0), ("c6", 4, 0), ("c6", 7, 0),
    ("c6", 8, 0),
)


def inverse_factor_block(block):
    n = block.shape[0]
    rows = lax.broadcasted_iota(jnp.int32, (n, n), 0)
    cols = lax.broadcasted_iota(jnp.int32, (n, n), 1)
    state = jnp.concatenate([block, jnp.where(rows == cols, 1.0, 0.0).astype(F32)], axis=1)
    row_in_group = lax.broadcasted_iota(jnp.int32, (8, 2 * n), 0)
    done = []
    for group in range(n // 8):
        left = n - 8 * group
        head = state[0:8, :]
        columns = [
            jnp.broadcast_to(state[:, 8 * group + j : 8 * group + j + 1], (left, 2 * n))
            for j in range(8)
        ]
        pivot_rows, pivot_cols = [], []
        for j in range(8):
            inv = lax.rsqrt(columns[j][j : j + 1, :])
            row = head[j : j + 1, :] * inv
            col = columns[j] * inv
            pivot_rows.append(row)
            pivot_cols.append(col)
            if j < 7:
                head = head - col[0:8] * row
            for later in range(j + 1, 8):
                columns[later] = columns[later] - col * col[later : later + 1, :]
        out = jnp.broadcast_to(pivot_rows[0], (8, 2 * n))
        for j in range(1, 8):
            out = jnp.where(row_in_group == j, pivot_rows[j], out)
        done.append(out)
        if left > 8:
            state = state[8:, :]
            for j in range(8):
                state = state - pivot_cols[j][8:] * pivot_rows[j]
    return jnp.concatenate(done, axis=0)[:, n:]


def factor_step(m_ref, step):
    k = m_ref.shape[0]
    lo, hi = step * BLOCK, (step + 1) * BLOCK
    inverse = inverse_factor_block(m_ref[lo:hi, lo:hi])
    rows = lax.broadcasted_iota(jnp.int32, (BLOCK, BLOCK), 0)
    cols = lax.broadcasted_iota(jnp.int32, (BLOCK, BLOCK), 1)
    m_ref[lo:hi, lo:hi] = jnp.where(rows == cols, 1.0, 0.0).astype(F32)
    panel = jnp.dot(inverse, m_ref[lo:hi, :], precision=HIGHEST, preferred_element_type=F32)
    m_ref[lo:hi, :] = panel
    if hi < k:
        m_ref[hi:, lo:hi] = jnp.zeros((k - hi, BLOCK), F32)
        m_ref[hi:, :] -= lax.dot_general(
            panel[:, hi:], panel, (((0,), (0,)), ((), ())),
            precision=HIGHEST, preferred_element_type=F32,
        )


def kernel(n_total, a_hbm, om_hbm, basis_hbm, total_hbm, inv_hbm,
           a_buf, om_buf, sketch, halves, to_core, from_core, part, total,
           folded, g_core, g_plane, g_line, g_sum, mat, basis_t, load_sem, out_sem, sems, *flat_bufs):
    rows_here, k = sketch.shape
    bufs = [flat_bufs[4 * i : 4 * i + 4] for i in range(len(CHUNKS))]
    wide, narrow = lax.axis_index("wide"), lax.axis_index("narrow")
    x, z = lax.rem(wide, NX), wide // NX
    y, c = narrow // 2, lax.rem(narrow, 2)

    def device(xx, yy, zz, cc):
        return (zz * NX + xx, yy * 2 + cc)

    sibling = device(x, y, z, 1 - c)
    on_x = [(lax.rem(x + d, NX), device(lax.rem(x + d, NX), y, z, c)) for d in range(1, NX)]
    on_y = [(lax.rem(y + d, NY), device(x, lax.rem(y + d, NY), z, c)) for d in range(1, NY)]
    on_z = [(lax.rem(z + d, NZ), device(x, y, lax.rem(z + d, NZ), c)) for d in range(1, NZ)]
    place = y * NX + x
    on_plane = []
    for d in range(1, NX * NY):
        other = lax.rem(place + d, NX * NY)
        on_plane.append((other, device(lax.rem(other, NX), other // NX, z, c)))

    used = [0]
    pending = []

    def exchange(size_like):
        at = used[0]
        used[0] += 2
        pending.append((at, size_like))
        return at

    def send(at, src, dst, to):
        pltpu.make_async_remote_copy(
            src_ref=src, dst_ref=dst, send_sem=sems.at[at], recv_sem=sems.at[at + 1],
            device_id=to, device_id_type=MESH,
        ).start()

    def wait_bytes(sem, like):
        pltpu.make_async_copy(like, like, sem).wait()

    def received(at, like):
        wait_bytes(sems.at[at + 1], like)

    barrier = pltpu.get_barrier_semaphore()
    partners = [sibling] + [to for _, to in on_plane] + [to for _, to in on_z]
    n_blocks, _, width = a_buf.shape
    loads = []
    for j in range(n_blocks):
        loads.append((
            pltpu.make_async_copy(a_hbm.at[:, pl.ds(j * width, width)], a_buf.at[j], load_sem.at[j]),
            pltpu.make_async_copy(om_hbm.at[:, pl.ds(j * width, width)], om_buf.at[j], load_sem.at[n_blocks + j]),
        ))
    for first, second in loads:
        first.start()
        second.start()
    for to in partners:
        pl.semaphore_signal(barrier, inc=1, device_id=to, device_id_type=MESH)

    for j in range(n_blocks):
        loads[j][0].wait()
        loads[j][1].wait()
        term = lax.dot_general(
            a_buf[j], om_buf[j], (((1,), (1,)), ((), ())), preferred_element_type=F32
        )
        if j == 0:
            sketch[...] = term
        else:
            sketch[...] += term

    value = sketch[...]
    high = value.astype(BF16)
    low = (value - high.astype(F32)).astype(BF16)
    halves[:, 0:rows_here] = high.T
    halves[:, rows_here:] = low.T

    def project(block, dst, at):
        cols = a_buf[block]
        res = jnp.dot(
            halves[...], jnp.concatenate([cols, cols], axis=0), preferred_element_type=F32
        )
        for t in range(NZ):
            dst[at, t] = res[:, t * LANES : (t + 1) * LANES]

    owners = [lax.rem(y + d, NY) for d in (2, 1, 3, 0)]
    ex_owner = []

    def to_sibling(o):
        project(2 * o + 1 - c, to_core, o)
        at = exchange(from_core.at[o])
        ex_owner.append(at)
        send(at, to_core.at[o], from_core.at[o], sibling)

    pl.semaphore_wait(barrier, len(partners))
    to_sibling(owners[0])

    gram = lax.dot_general(
        sketch[...], sketch[...], (((0,), (0,)), ((), ())),
        precision=HIGHEST, preferred_element_type=F32,
    )
    folded[...] = jnp.zeros(folded.shape, F32)
    folded[0:128, 0:k] = gram[0:128, :]
    folded[128:256, 0 : k - 128] = gram[128:256, 128:]
    folded[128 : k - 128, 256 : k] = gram[256:, 256:]
    half_rows = g_core.shape[0]
    mine = pl.multiple_of(c * half_rows, 8)
    yours = pl.multiple_of((1 - c) * half_rows, 8)
    ex_core = exchange(g_core)
    send(ex_core, folded.at[pl.ds(yours, half_rows)], g_core, sibling)

    for o in owners[1:]:
        to_sibling(o)
    received(ex_core, g_core)
    folded[pl.ds(mine, half_rows)] += g_core[...]
    my_tile = pl.multiple_of(c * half_rows + place * 8, 8)
    ex_plane = exchange(g_plane)
    for d, (other, to) in enumerate(on_plane):
        src = folded.at[pl.ds(pl.multiple_of(c * half_rows + other * 8, 8), 8)]
        send(ex_plane, src, g_plane.at[d], to)

    half = NZ // 2

    def rows_of(ch):
        return pl.ds(CHUNKS[ch][1], CHUNKS[ch][2])

    def quarter(ch, d):
        q = CHUNKS[ch][2] // NX
        return pl.ds(pl.multiple_of(CHUNKS[ch][1] + lax.rem(x + d, NX) * q, 8), q)

    flying = {}

    def began(name, ch, like, i=0):
        at = exchange(like)
        flying[name, ch, i] = (at, like)
        return at

    def arrived(name, ch, i=0):
        received(*flying[name, ch, i])

    def summed(buf, n):
        acc = buf[0]
        for d in range(1, n):
            acc = acc + buf[d]
        return acc

    def owner(ch, i):
        o = owners[i]
        project(2 * o + c, part, o)
        received(ex_owner[i], from_core.at[o])

        def add(t, carry):
            part[o, t] += from_core[o, t]
            return carry

        lax.fori_loop(0, NZ, add, 0)

    def ya(ch, i):
        buf, rows = bufs[ch][0], rows_of(ch)
        at = began("a", ch, buf)
        send(at, part.at[owners[0], 0:half, rows, :], buf.at[0], on_y[0][1])
        send(at, part.at[owners[0], half:NZ, rows, :], buf.at[1], on_y[2][1])

    def yb(ch, i):
        arrived("a", ch)
        old, buf, rows = bufs[ch][0], bufs[ch][1], rows_of(ch)
        part[owners[1], 0:half, rows, :] += old[0]
        part[owners[2], half:NZ, rows, :] += old[1]
        at = began("b", ch, buf)
        send(at, part.at[owners[1], :, rows, :], buf.at[0], on_y[0][1])
        send(at, part.at[owners[2], :, rows, :], buf.at[1], on_y[2][1])

    def y2(ch, i):
        arrived("b", ch)
        old, buf, rows = bufs[ch][1], bufs[ch][2], rows_of(ch)
        part[y, :, rows, :] += old[0] + old[1]
        at = began("2", ch, buf)
        for d in range(1, NX):
            send(at, part.at[y, :, quarter(ch, d), :], buf.at[d - 1], on_x[d - 1][1])

    def y3(ch, i):
        arrived("2", ch)
        old, buf, rows = bufs[ch][2], bufs[ch][3], quarter(ch, 0)
        part[y, :, rows, :] += summed(old, 3)
        at = began("3", ch, buf)
        for d, (zz, to) in enumerate(on_z):
            send(at, part.at[y, zz, rows, :], buf.at[d], to)

    def xa(ch, i):
        buf, rows = bufs[ch][0], quarter(ch, 2)
        at = began("a", ch, buf.at[i], i)
        send(at, part.at[owners[i], 0:half, rows, :], buf.at[i, 0], on_x[0][1])
        send(at, part.at[owners[i], half:NZ, rows, :], buf.at[i, 1], on_x[2][1])

    def xb(ch, i):
        arrived("a", ch, i)
        old, buf = bufs[ch][0], bufs[ch][1]
        up, down = quarter(ch, 1), quarter(ch, 3)
        part[owners[i], 0:half, up, :] += old[i, 0]
        part[owners[i], half:NZ, down, :] += old[i, 1]
        at = began("b", ch, buf.at[i], i)
        send(at, part.at[owners[i], :, up, :], buf.at[i, 0], on_x[0][1])
        send(at, part.at[owners[i], :, down, :], buf.at[i, 1], on_x[2][1])

    def x2(ch, i):
        old, buf, rows = bufs[ch][1], bufs[ch][2], quarter(ch, 0)
        for j in range(NY):
            arrived("b", ch, j)
            part[owners[j], :, rows, :] += old[j, 0] + old[j, 1]
        at = began("2", ch, buf)
        for d, (yy, to) in enumerate(on_y):
            send(at, part.at[yy, :, rows, :], buf.at[d], to)

    x3 = y3

    def za(ch, i):
        buf, rows = bufs[ch][0], rows_of(ch)
        at = began("a", ch, buf.at[i], i)
        for d, (zz, to) in enumerate(on_z):
            send(at, part.at[owners[i], zz, rows, :], buf.at[i, d], to)

    def z2(ch, i):
        old, buf, rows = bufs[ch][0], bufs[ch][2], rows_of(ch)
        for j in range(NY):
            arrived("a", ch, j)
            part[owners[j], z, rows, :] += summed(old.at[j], NZ - 1)
        at = began("2", ch, buf)
        for d, (yy, to) in enumerate(on_y):
            send(at, part.at[yy, z, rows, :], buf.at[d], to)

    def z3(ch, i):
        arrived("2", ch)
        old, buf, rows = bufs[ch][2], bufs[ch][3], rows_of(ch)
        part[y, z, rows, :] += summed(old, 3)
        at = began("3", ch, buf)
        for d in range(1, NX):
            send(at, part.at[y, z, quarter(ch, d), :], buf.at[d - 1], on_x[d - 1][1])

    def c4(ch, i):
        arrived("3", ch)
        old, rows, q = bufs[ch][3], quarter(ch, 0), CHUNKS[ch][2] // NX
        total[z, rows, :] = part[y, z, rows, :] + summed(old, old.shape[0])
        line = on_x if CHUNKS[ch][3] else on_z
        at = began("4", ch, total.at[0 : len(line), 0:q, :])
        for _, to in line:
            send(at, total.at[z, rows, :], total.at[z, rows, :], to)

    def c5(ch, i):
        arrived("4", ch)
        n = CHUNKS[ch][2]
        if CHUNKS[ch][3]:
            at = began("5", ch, total.at[0 : NZ - 1, 0:n, :])
            for _, to in on_z:
                send(at, total.at[z, rows_of(ch), :], total.at[z, rows_of(ch), :], to)
        else:
            at = began("5", ch, total.at[:, 0 : 3 * n // NX, :])
            for _, to in on_x:
                send(at, total.at[:, quarter(ch, 0), :], total.at[:, quarter(ch, 0), :], to)

    outs = []

    def c6(ch, i):
        arrived("5", ch)
        copy = pltpu.make_async_copy(
            total.at[:, rows_of(ch), :], total_hbm.at[:, rows_of(ch), :], out_sem.at[2 + ch]
        )
        copy.start()
        outs.append(copy)

    tile = pl.ds(my_tile, 8)

    def gram_line(ch, i):
        received(ex_plane, g_plane)
        g_line[z] = folded[tile, :] + summed(g_plane, NX * NY - 1)
        at = began("g", -1, g_plane.at[0 : NZ - 1])
        for _, to in on_z:
            send(at, g_line.at[z], g_line.at[z], to)

    def gram_spread(ch, i):
        arrived("g", -1)
        g_sum[tile, :] = summed(g_line, NZ)
        at = began("h", -1, g_plane)
        for _, to in on_plane:
            send(at, g_sum.at[tile], g_sum.at[tile], to)

    def gram_core(ch, i):
        arrived("h", -1)
        at = began("i", -1, g_core)
        my_half = pl.ds(mine, half_rows)
        send(at, g_sum.at[my_half], g_sum.at[my_half], sibling)

    def gram_ready(ch, i):
        arrived("i", -1)
        mat[0:128, :] = g_sum[0:128, 0:k]
        mat[128:256, 128:] = g_sum[128:256, 0 : k - 128]
        mat[256:, 256:] = g_sum[128 : k - 128, 256 : k]

    def factor(ch, i):
        factor_step(mat, i)

    def basis(ch, i):
        rows = lax.broadcasted_iota(jnp.int32, (k, k), 0)
        cols = lax.broadcasted_iota(jnp.int32, (k, k), 1)
        mat[...] = jnp.where(rows >= cols, mat[...], 0.0)
        basis_t[...] = lax.dot_general(
            mat[...], sketch[...], (((1,), (1,)), ((), ())),
            precision=HIGHEST, preferred_element_type=F32,
        ) * math.sqrt(n_total)
        for j, (src, dst) in enumerate(((mat, inv_hbm), (basis_t, basis_hbm))):
            copy = pltpu.make_async_copy(src, dst, out_sem.at[j])
            copy.start()
            outs.append(copy)

    steps = dict(
        owner=owner, ya=ya, yb=yb, y2=y2, y3=y3, xa=xa, xb=xb, x2=x2, x3=x3, za=za, z2=z2, z3=z3,
        c4=c4, c5=c5, c6=c6, gram_line=gram_line, gram_spread=gram_spread, gram_core=gram_core,
        gram_ready=gram_ready, factor=factor, basis=basis,
    )
    for name, ch, i in ORDER:
        steps[name](ch, i)
    for copy in outs:
        copy.wait()
    for at, like in pending:
        wait_bytes(sems.at[at], like)


def finish_kernel(n_total, basis_in, total_ref, inv_ref, basis_out, coef_ref):
    basis_out[...] = basis_in[...]
    both = jnp.concatenate([total_ref[0], total_ref[1]], axis=1)
    coef_ref[...] = jnp.dot(
        inv_ref[...], both, precision=HIGHEST, preferred_element_type=F32
    ) * (1.0 / math.sqrt(n_total))


def per_device(activations, test_matrix):
    rows, d = activations.shape
    k = test_matrix.shape[1]
    n_total = rows * lax.axis_size("wide") * lax.axis_size("narrow")
    width = d // (2 * NY)
    bufs = []
    half = NZ // 2
    for axis, _, n, _ in CHUNKS:
        q = n // NX
        if axis == "y":
            shapes = ((2, half, n, LANES), (2, NZ, n, LANES), (3, NZ, q, LANES), (7, q, LANES))
        elif axis == "x":
            shapes = (
                (NY, 2, half, q, LANES), (NY, 2, NZ, q, LANES), (3, NZ, q, LANES), (7, q, LANES)
            )
        else:
            shapes = ((NY, 7, n, LANES), (8, LANES), (3, n, LANES), (3, q, LANES))
        bufs += [pltpu.VMEM(s, F32) for s in shapes]
    block = (NY, NZ, k, LANES)
    hbm = pl.BlockSpec(memory_space=pl.ANY)
    basis_t, total, inverse = pl.pallas_call(
        functools.partial(kernel, n_total),
        out_shape=(
            jax.ShapeDtypeStruct((k, rows), F32),
            jax.ShapeDtypeStruct((NZ, k, LANES), F32),
            jax.ShapeDtypeStruct((k, k), F32),
        ),
        in_specs=[hbm] * 2,
        out_specs=(hbm, hbm, hbm),
        scratch_shapes=[
            pltpu.VMEM((d // width, rows, width), BF16),
            pltpu.VMEM((d // width, k, width), BF16),
            pltpu.VMEM((rows, k), F32),
            pltpu.VMEM((k, 2 * rows), BF16),
            pltpu.VMEM(block, F32),
            pltpu.VMEM(block, F32),
            pltpu.VMEM(block, F32),
            pltpu.VMEM((NZ, k, LANES), F32),
            pltpu.VMEM((256, 384), F32),
            pltpu.VMEM((128, 384), F32),
            pltpu.VMEM((NX * NY - 1, 8, 384), F32),
            pltpu.VMEM((NZ, 8, 384), F32),
            pltpu.VMEM((256, 384), F32),
            pltpu.VMEM((k, k), F32),
            pltpu.VMEM((k, rows), F32),
            pltpu.SemaphoreType.DMA((2 * d // width,)),
            pltpu.SemaphoreType.DMA((2 + len(CHUNKS),)),
            pltpu.SemaphoreType.DMA((SEMAPHORES,)),
        ] + bufs,
        compiler_params=pltpu.CompilerParams(
            collective_id=0, has_side_effects=True, vmem_limit_bytes=56 * 1024 * 1024
        ),
        name="range_finder",
    )(activations, test_matrix.T)
    steps = NZ // 2
    by_columns = pl.BlockSpec((k, rows // steps), lambda i: (0, i))
    basis_t, coeffs = pl.pallas_call(
        functools.partial(finish_kernel, n_total),
        grid=(steps,),
        out_shape=(
            jax.ShapeDtypeStruct((k, rows), F32),
            jax.ShapeDtypeStruct((k, width), F32),
        ),
        in_specs=[
            by_columns,
            pl.BlockSpec((2, k, LANES), lambda i: (i, 0, 0)),
            pl.BlockSpec((k, k), lambda i: (0, 0)),
        ],
        out_specs=(by_columns, pl.BlockSpec((k, 2 * LANES), lambda i: (0, i))),
        name="apply_inverse",
    )(basis_t, total, inverse)
    return basis_t.T, coeffs


def solution(mesh):
    return jax.shard_map(
        per_device,
        mesh=mesh,
        in_specs=(P(("wide", "narrow"), None), P()),
        out_specs=(P(("wide", "narrow"), None), P(None, "narrow")),
        check_vma=False,
    )
```

```python
import functools
import math

import jax
import jax.numpy as jnp
from jax import lax
from jax.experimental import pallas as pl
from jax.experimental.pallas import tpu as pltpu
from jax.sharding import PartitionSpec as P

MESH = pl.DeviceIdType.MESH
HIGHEST = lax.Precision.HIGHEST
F32 = jnp.float32
BF16 = jnp.bfloat16
NX, NY, NZ = 4, 4, 8
BLOCK = 64
LANES = 128
SEMAPHORES = 176
BEFORE_GRAM = 3

CHUNKS = (
    ("y", 0, 32, True),
    ("x", 32, 32, False),
    ("x", 64, 32, False),
    ("y", 96, 32, False),
    ("y", 128, 32, True),
    ("x", 160, 32, False),
    ("z", 192, 32, False),
    ("x", 224, 32, False),
    ("z", 256, 32, False),
    ("y", 288, 32, True),
)

ORDER = (
    ("ya", 0), ("xa", 1), ("xa", 2), ("gram_plane", -1), ("ya", 3), ("ya", 4), ("xa", 5), ("yb", 0),
    ("xb", 1), ("za", 6), ("xa", 7), ("xb", 2), ("za", 8), ("yb", 3), ("gram_line", -1), ("ya", 9), ("yb", 4),
    ("xb", 5), ("y2", 0), ("zb", 6), ("x2", 1), ("xb", 7), ("y2", 3), ("zb", 8), ("yb", 9), ("x2", 2),
    ("gram_spread", -1), ("y2", 4), ("x2", 5), ("y3", 1), ("y3", 0), ("z2", 6), ("y2", 9), ("x2", 7),
    ("y3", 2), ("y3", 3), ("z2", 8), ("gram_core", -1), ("y3", 5), ("y3", 4), ("z3", 6), ("c4", 1), ("c4", 0),
    ("gram_ready", -1), ("y3", 7), ("y3", 9), ("factor", 0), ("c4", 2), ("z3", 8), ("factor", 1), ("c4", 3),
    ("c4", 6), ("factor", 2), ("c4", 5), ("c5", 0), ("c4", 4), ("factor", 3), ("c5", 1), ("c4", 7), ("c4", 8),
    ("factor", 4), ("c4", 9), ("c5", 2), ("factor", 5), ("c5", 3), ("c5", 4), ("c5", 6), ("factor", 6),
    ("c5", 5), ("factor", 7), ("c6", 1), ("c5", 9), ("factor", 8), ("factor", 9), ("c5", 7), ("c6", 0),
    ("c6", 2), ("factor", 10), ("c6", 3), ("c5", 8), ("factor", 11), ("c6", 6), ("factor", 12),
    ("factor", 13), ("c6", 5), ("c6", 4), ("factor", 14), ("basis", -1), ("c6", 7), ("c6", 9), ("c6", 8),
)


def eliminate(state, first, last):
    width = state.shape[1]
    row_in_group = lax.broadcasted_iota(jnp.int32, (8, width), 0)
    done = []
    for group in range(first, last):
        left = state.shape[0]
        head = state[0:8, :]
        columns = [
            jnp.broadcast_to(state[:, 8 * group + j : 8 * group + j + 1], (left, width))
            for j in range(8)
        ]
        pivot_rows, pivot_cols = [], []
        for j in range(8):
            inv = lax.rsqrt(columns[j][j : j + 1, :])
            row = head[j : j + 1, :] * inv
            col = columns[j] * inv
            pivot_rows.append(row)
            pivot_cols.append(col)
            if j < 7:
                head = head - col[0:8] * row
            for later in range(j + 1, 8):
                columns[later] = columns[later] - col * col[later : later + 1, :]
        out = jnp.broadcast_to(pivot_rows[0], (8, width))
        for j in range(1, 8):
            out = jnp.where(row_in_group == j, pivot_rows[j], out)
        done.append(out)
        if left > 8:
            state = state[8:, :]
            for j in range(8):
                state = state - pivot_cols[j][8:] * pivot_rows[j]
    return jnp.concatenate(done, axis=0), state


def factor_step(m_ref, block_ref, step, phase):
    k = m_ref.shape[0]
    lo, hi = step * BLOCK, (step + 1) * BLOCK
    half, groups = BLOCK // 2, BLOCK // 8
    rows = lax.broadcasted_iota(jnp.int32, (BLOCK, BLOCK), 0)
    cols = lax.broadcasted_iota(jnp.int32, (BLOCK, BLOCK), 1)
    identity = jnp.where(rows == cols, 1.0, 0.0).astype(F32)
    if phase == 0:
        state = jnp.concatenate([m_ref[lo:hi, lo:hi], identity], axis=1)
        block_ref[0:half, :], block_ref[half:, :] = eliminate(state, 0, groups // 2)
    elif phase == 1:
        done, _ = eliminate(block_ref[half:, :], groups // 2, groups)
        inverse = jnp.concatenate([block_ref[0:half, BLOCK:], done[:, BLOCK:]], axis=0)
        m_ref[lo:hi, lo:hi] = identity
        m_ref[lo:hi, :] = jnp.dot(
            inverse, m_ref[lo:hi, :], precision=HIGHEST, preferred_element_type=F32
        )
    elif hi < k:
        panel = m_ref[lo:hi, :]
        m_ref[hi:, lo:hi] = jnp.zeros((k - hi, BLOCK), F32)
        m_ref[hi:, :] -= lax.dot_general(
            panel[:, hi:], panel, (((0,), (0,)), ((), ())),
            precision=HIGHEST, preferred_element_type=F32,
        )


def kernel(n_total, a_hbm, om_hbm, basis_hbm, total_hbm, inv_hbm,
           a_buf, om_buf, sketch, halves, to_core, from_core, part, total,
           folded, g_core, g_plane, g_line, g_sum, mat, block, basis_t, load_sem, out_sem, sems, *flat_bufs):
    k, rows_here = sketch.shape
    bufs = [flat_bufs[4 * i : 4 * i + 4] for i in range(len(CHUNKS))]
    wide, narrow = lax.axis_index("wide"), lax.axis_index("narrow")
    x, z = lax.rem(wide, NX), wide // NX
    y, c = narrow // 2, lax.rem(narrow, 2)

    def device(xx, yy, zz, cc):
        return (zz * NX + xx, yy * 2 + cc)

    sibling = device(x, y, z, 1 - c)
    on_x = [(lax.rem(x + d, NX), device(lax.rem(x + d, NX), y, z, c)) for d in range(1, NX)]
    on_y = [(lax.rem(y + d, NY), device(x, lax.rem(y + d, NY), z, c)) for d in range(1, NY)]
    on_z = [(lax.rem(z + d, NZ), device(x, y, lax.rem(z + d, NZ), c)) for d in range(1, NZ)]
    place = y * NX + x
    on_plane = []
    for d in range(1, NX * NY):
        other = lax.rem(place + d, NX * NY)
        on_plane.append((other, device(lax.rem(other, NX), other // NX, z, c)))

    used = [0]
    pending = []

    def exchange(size_like):
        at = used[0]
        used[0] += 2
        pending.append((at, size_like))
        return at

    def send(at, src, dst, to):
        pltpu.make_async_remote_copy(
            src_ref=src, dst_ref=dst, send_sem=sems.at[at], recv_sem=sems.at[at + 1],
            device_id=to, device_id_type=MESH,
        ).start()

    def wait_bytes(sem, like):
        pltpu.make_async_copy(like, like, sem).wait()

    def received(at, like):
        wait_bytes(sems.at[at + 1], like)

    barrier = pltpu.get_barrier_semaphore()
    partners = [sibling] + [to for _, to in on_plane] + [to for _, to in on_z]
    n_blocks, _, width = a_buf.shape
    loads = []
    for j in range(n_blocks):
        loads.append((
            pltpu.make_async_copy(a_hbm.at[:, pl.ds(j * width, width)], a_buf.at[j], load_sem.at[j]),
            pltpu.make_async_copy(om_hbm.at[:, pl.ds(j * width, width)], om_buf.at[j], load_sem.at[n_blocks + j]),
        ))
    for first, second in loads:
        first.start()
        second.start()
    for to in partners:
        pl.semaphore_signal(barrier, inc=1, device_id=to, device_id_type=MESH)

    for j in range(n_blocks):
        loads[j][0].wait()
        loads[j][1].wait()
        term = lax.dot_general(
            om_buf[j], a_buf[j], (((1,), (1,)), ((), ())), preferred_element_type=F32
        )
        if j == 0:
            sketch[...] = term
        else:
            sketch[...] += term

    value = sketch[...]
    high = value.astype(BF16)
    low = (value - high.astype(F32)).astype(BF16)
    halves[:, 0:rows_here] = high
    halves[:, rows_here:] = low

    def project(block, dst, at):
        cols = a_buf[block]
        res = jnp.dot(
            halves[...], jnp.concatenate([cols, cols], axis=0), preferred_element_type=F32
        )
        for t in range(NZ):
            dst[at, t] = res[:, t * LANES : (t + 1) * LANES]

    pl.semaphore_wait(barrier, len(partners))
    for o in range(NY):
        project(2 * o + 1 - c, to_core, o)
    ex_chunk = []

    def to_sibling(chunks):
        for _, first, n, _ in chunks:
            rows = pl.ds(first, n)
            at = exchange(from_core.at[:, :, rows, :])
            ex_chunk.append(at)
            send(at, to_core.at[:, :, rows, :], from_core.at[:, :, rows, :], sibling)

    to_sibling(CHUNKS[:BEFORE_GRAM])

    gram = lax.dot_general(
        sketch[...], sketch[...], (((1,), (1,)), ((), ())),
        precision=HIGHEST, preferred_element_type=F32,
    )
    folded[...] = jnp.zeros(folded.shape, F32)
    folded[0:128, 0:k] = gram[0:128, :]
    folded[128:256, 0 : k - 128] = gram[128:256, 128:]
    folded[128 : k - 128, 256 : k] = gram[256:, 256:]
    half_rows = g_core.shape[0]
    mine = pl.multiple_of(c * half_rows, 8)
    yours = pl.multiple_of((1 - c) * half_rows, 8)
    ex_core = exchange(g_core)
    send(ex_core, folded.at[pl.ds(yours, half_rows)], g_core, sibling)
    to_sibling(CHUNKS[BEFORE_GRAM:])
    for o in range(NY):
        project(2 * o + c, part, o)

    my_tile = pl.multiple_of(c * half_rows + place * 8, 8)

    half = NZ // 2

    def rows_of(ch):
        return pl.ds(CHUNKS[ch][1], CHUNKS[ch][2])

    def quarter(ch, d):
        q = CHUNKS[ch][2] // NX
        return pl.ds(pl.multiple_of(CHUNKS[ch][1] + lax.rem(x + d, NX) * q, 8), q)

    flying = {}

    def began(name, ch, like):
        at = exchange(like)
        flying[name, ch] = (at, like)
        return at

    def arrived(name, ch):
        received(*flying[name, ch])

    def summed(buf, n):
        acc = buf[0]
        for d in range(1, n):
            acc = acc + buf[d]
        return acc

    def from_sibling(ch):
        rows = rows_of(ch)
        received(ex_chunk[ch], from_core.at[:, :, rows, :])

        def add(o, carry):
            part[o, :, rows, :] += from_core[o, :, rows, :]
            return carry

        lax.fori_loop(0, NY, add, 0)

    far, up_y, down_y = [lax.rem(y + d, NY) for d in (2, 1, 3)]

    def ya(ch):
        from_sibling(ch)
        buf, rows = bufs[ch][0], rows_of(ch)
        at = began("a", ch, buf)
        send(at, part.at[far, 0:half, rows, :], buf.at[0], on_y[0][1])
        send(at, part.at[far, half:NZ, rows, :], buf.at[1], on_y[2][1])

    def yb(ch):
        arrived("a", ch)
        old, buf, rows = bufs[ch][0], bufs[ch][1], rows_of(ch)
        part[up_y, 0:half, rows, :] += old[0]
        part[down_y, half:NZ, rows, :] += old[1]
        at = began("b", ch, buf)
        send(at, part.at[up_y, :, rows, :], buf.at[0], on_y[0][1])
        send(at, part.at[down_y, :, rows, :], buf.at[1], on_y[2][1])

    def y2(ch):
        arrived("b", ch)
        old, buf, rows = bufs[ch][1], bufs[ch][2], rows_of(ch)
        part[y, :, rows, :] += old[0] + old[1]
        at = began("2", ch, buf)
        for d in range(1, NX):
            send(at, part.at[y, :, quarter(ch, d), :], buf.at[d - 1], on_x[d - 1][1])

    def y3(ch):
        arrived("2", ch)
        old, buf, rows = bufs[ch][2], bufs[ch][3], quarter(ch, 0)
        part[y, :, rows, :] += summed(old, 3)
        at = began("3", ch, buf)
        for d, (zz, to) in enumerate(on_z):
            send(at, part.at[y, zz, rows, :], buf.at[d], to)

    def xa(ch):
        from_sibling(ch)
        buf, rows = bufs[ch][0], quarter(ch, 2)
        at = began("a", ch, buf)
        send(at, part.at[:, 0:half, rows, :], buf.at[0], on_x[0][1])
        send(at, part.at[:, half:NZ, rows, :], buf.at[1], on_x[2][1])

    def xb(ch):
        arrived("a", ch)
        old, buf = bufs[ch][0], bufs[ch][1]
        up, down = quarter(ch, 1), quarter(ch, 3)
        part[:, 0:half, up, :] += old[0]
        part[:, half:NZ, down, :] += old[1]
        at = began("b", ch, buf)
        send(at, part.at[:, :, up, :], buf.at[0], on_x[0][1])
        send(at, part.at[:, :, down, :], buf.at[1], on_x[2][1])

    def x2(ch):
        arrived("b", ch)
        old, buf, rows = bufs[ch][1], bufs[ch][2], quarter(ch, 0)
        part[:, :, rows, :] += old[0] + old[1]
        at = began("2", ch, buf)
        for d, (yy, to) in enumerate(on_y):
            send(at, part.at[yy, :, rows, :], buf.at[d], to)

    def away(d):
        return lax.rem(z + d, NZ), on_z[d - 1][1]

    def za(ch):
        from_sibling(ch)
        buf, rows = bufs[ch][0], rows_of(ch)
        at = began("a", ch, buf)
        send(at, part.at[:, away(5)[0], rows, :], buf.at[0], away(7)[1])
        send(at, part.at[:, away(3)[0], rows, :], buf.at[1], away(1)[1])
        send(at, part.at[0:2, away(4)[0], rows, :], buf.at[2, 0:2], away(2)[1])
        send(at, part.at[2:NY, away(4)[0], rows, :], buf.at[2, 2:NY], away(6)[1])

    def zb(ch):
        arrived("a", ch)
        old, buf, rows = bufs[ch][0], bufs[ch][1], rows_of(ch)
        down, up = away(6)[0], away(2)[0]
        part[:, down, rows, :] += old[0]
        part[2:NY, down, rows, :] += old[2, 2:NY]
        part[:, up, rows, :] += old[1]
        part[0:2, up, rows, :] += old[2, 0:2]
        at = began("b", ch, buf)
        for slot, d in enumerate((1, 7, 2, 6)):
            zz, to = away(d)
            send(at, part.at[:, zz, rows, :], buf.at[slot], to)

    def z2(ch):
        arrived("b", ch)
        old, buf, rows = bufs[ch][1], bufs[ch][2], rows_of(ch)
        part[:, z, rows, :] += summed(old, 4)
        at = began("2", ch, buf)
        for d, (yy, to) in enumerate(on_y):
            send(at, part.at[yy, z, rows, :], buf.at[d], to)

    def z3(ch):
        arrived("2", ch)
        old, buf, rows = bufs[ch][2], bufs[ch][3], rows_of(ch)
        part[y, z, rows, :] += summed(old, 3)
        at = began("3", ch, buf)
        for d in range(1, NX):
            send(at, part.at[y, z, quarter(ch, d), :], buf.at[d - 1], on_x[d - 1][1])

    def c4(ch):
        arrived("3", ch)
        old, rows, q = bufs[ch][3], quarter(ch, 0), CHUNKS[ch][2] // NX
        total[z, rows, :] = part[y, z, rows, :] + summed(old, old.shape[0])
        line = on_x if CHUNKS[ch][3] else on_z
        at = began("4", ch, total.at[0 : len(line), 0:q, :])
        for _, to in line:
            send(at, total.at[z, rows, :], total.at[z, rows, :], to)

    def c5(ch):
        arrived("4", ch)
        n = CHUNKS[ch][2]
        if CHUNKS[ch][3]:
            at = began("5", ch, total.at[0 : NZ - 1, 0:n, :])
            for _, to in on_z:
                send(at, total.at[z, rows_of(ch), :], total.at[z, rows_of(ch), :], to)
        else:
            at = began("5", ch, total.at[:, 0 : 3 * n // NX, :])
            for _, to in on_x:
                send(at, total.at[:, quarter(ch, 0), :], total.at[:, quarter(ch, 0), :], to)

    outs = []

    def c6(ch):
        arrived("5", ch)
        copy = pltpu.make_async_copy(
            total.at[:, rows_of(ch), :], total_hbm.at[:, rows_of(ch), :], out_sem.at[2 + ch]
        )
        copy.start()
        outs.append(copy)

    tile = pl.ds(my_tile, 8)

    def gram_plane(ch):
        received(ex_core, g_core)
        folded[pl.ds(mine, half_rows)] += g_core[...]
        at = began("f", -1, g_plane)
        for d, (other, to) in enumerate(on_plane):
            src = folded.at[pl.ds(pl.multiple_of(c * half_rows + other * 8, 8), 8)]
            send(at, src, g_plane.at[d], to)

    def gram_line(ch):
        arrived("f", -1)
        g_line[z] = folded[tile, :] + summed(g_plane, NX * NY - 1)
        at = began("g", -1, g_plane.at[0 : NZ - 1])
        for _, to in on_z:
            send(at, g_line.at[z], g_line.at[z], to)

    def gram_spread(ch):
        arrived("g", -1)
        g_sum[tile, :] = summed(g_line, NZ)
        at = began("h", -1, g_plane)
        for _, to in on_plane:
            send(at, g_sum.at[tile], g_sum.at[tile], to)

    def gram_core(ch):
        arrived("h", -1)
        at = began("i", -1, g_core)
        my_half = pl.ds(mine, half_rows)
        send(at, g_sum.at[my_half], g_sum.at[my_half], sibling)

    def gram_ready(ch):
        arrived("i", -1)
        mat[0:128, :] = g_sum[0:128, 0:k]
        mat[128:256, 128:] = g_sum[128:256, 0 : k - 128]
        mat[256:, 256:] = g_sum[128 : k - 128, 256 : k]

    def factor(i):
        factor_step(mat, block, i // 3, i % 3)

    def basis(ch):
        rows = lax.broadcasted_iota(jnp.int32, (k, k), 0)
        cols = lax.broadcasted_iota(jnp.int32, (k, k), 1)
        mat[...] = jnp.where(rows >= cols, mat[...], 0.0)
        basis_t[...] = jnp.dot(
            mat[...], sketch[...], precision=HIGHEST, preferred_element_type=F32
        ) * math.sqrt(n_total)
        for j, (src, dst) in enumerate(((mat, inv_hbm), (basis_t, basis_hbm))):
            copy = pltpu.make_async_copy(src, dst, out_sem.at[j])
            copy.start()
            outs.append(copy)

    steps = dict(
        ya=ya, yb=yb, y2=y2, y3=y3, xa=xa, xb=xb, x2=x2, za=za, zb=zb, z2=z2, z3=z3, c4=c4, c5=c5, c6=c6,
        gram_plane=gram_plane, gram_line=gram_line, gram_spread=gram_spread, gram_core=gram_core,
        gram_ready=gram_ready, factor=factor, basis=basis,
    )
    for name, arg in ORDER:
        steps[name](arg)
    for copy in outs:
        copy.wait()
    for at, like in pending:
        wait_bytes(sems.at[at], like)


def finish_kernel(n_total, basis_in, total_ref, inv_ref, basis_out, coef_ref):
    basis_out[...] = basis_in[...]
    both = jnp.concatenate([total_ref[0], total_ref[1]], axis=1)
    coef_ref[...] = jnp.dot(
        inv_ref[...], both, precision=HIGHEST, preferred_element_type=F32
    ) * (1.0 / math.sqrt(n_total))


def per_device(activations, test_matrix):
    rows, d = activations.shape
    k = test_matrix.shape[1]
    n_total = rows * lax.axis_size("wide") * lax.axis_size("narrow")
    width = d // (2 * NY)
    bufs = []
    half = NZ // 2
    for axis, _, n, _ in CHUNKS:
        q = n // NX
        if axis == "y":
            shapes = ((2, half, n, LANES), (2, NZ, n, LANES), (3, NZ, q, LANES), (7, q, LANES))
        elif axis == "x":
            shapes = (
                (2, NY, half, q, LANES), (2, NY, NZ, q, LANES), (3, NZ, q, LANES), (7, q, LANES)
            )
        else:
            shapes = ((3, NY, n, LANES), (4, NY, n, LANES), (3, n, LANES), (3, q, LANES))
        bufs += [pltpu.VMEM(s, F32) for s in shapes]
    block = (NY, NZ, k, LANES)
    hbm = pl.BlockSpec(memory_space=pl.ANY)
    basis_t, total, inverse = pl.pallas_call(
        functools.partial(kernel, n_total),
        out_shape=(
            jax.ShapeDtypeStruct((k, rows), F32),
            jax.ShapeDtypeStruct((NZ, k, LANES), F32),
            jax.ShapeDtypeStruct((k, k), F32),
        ),
        in_specs=[hbm] * 2,
        out_specs=(hbm, hbm, hbm),
        scratch_shapes=[
            pltpu.VMEM((d // width, rows, width), BF16),
            pltpu.VMEM((d // width, k, width), BF16),
            pltpu.VMEM((k, rows), F32),
            pltpu.VMEM((k, 2 * rows), BF16),
            pltpu.VMEM(block, F32),
            pltpu.VMEM(block, F32),
            pltpu.VMEM(block, F32),
            pltpu.VMEM((NZ, k, LANES), F32),
            pltpu.VMEM((256, 384), F32),
            pltpu.VMEM((128, 384), F32),
            pltpu.VMEM((NX * NY - 1, 8, 384), F32),
            pltpu.VMEM((NZ, 8, 384), F32),
            pltpu.VMEM((256, 384), F32),
            pltpu.VMEM((k, k), F32),
            pltpu.VMEM((BLOCK, 2 * BLOCK), F32),
            pltpu.VMEM((k, rows), F32),
            pltpu.SemaphoreType.DMA((2 * d // width,)),
            pltpu.SemaphoreType.DMA((2 + len(CHUNKS),)),
            pltpu.SemaphoreType.DMA((SEMAPHORES,)),
        ] + bufs,
        compiler_params=pltpu.CompilerParams(
            collective_id=0, has_side_effects=True, vmem_limit_bytes=56 * 1024 * 1024
        ),
        name="range_finder",
    )(activations, test_matrix.T)
    steps = NZ // 2
    by_columns = pl.BlockSpec((k, rows // steps), lambda i: (0, i))
    basis_t, coeffs = pl.pallas_call(
        functools.partial(finish_kernel, n_total),
        grid=(steps,),
        out_shape=(
            jax.ShapeDtypeStruct((k, rows), F32),
            jax.ShapeDtypeStruct((k, width), F32),
        ),
        in_specs=[
            by_columns,
            pl.BlockSpec((2, k, LANES), lambda i: (i, 0, 0)),
            pl.BlockSpec((k, k), lambda i: (0, 0)),
        ],
        out_specs=(by_columns, pl.BlockSpec((k, 2 * LANES), lambda i: (0, i))),
        name="apply_inverse",
    )(basis_t, total, inverse)
    return basis_t.T, coeffs


def solution(mesh):
    return jax.shard_map(
        per_device,
        mesh=mesh,
        in_specs=(P(("wide", "narrow"), None), P()),
        out_specs=(P(("wide", "narrow"), None), P(None, "narrow")),
        check_vma=False,
    )
```

```python
import functools
import math

import jax
import jax.numpy as jnp
from jax import lax
from jax.experimental import pallas as pl
from jax.experimental.pallas import tpu as pltpu
from jax.sharding import PartitionSpec as P

MESH = pl.DeviceIdType.MESH
HIGHEST = lax.Precision.HIGHEST
F32 = jnp.float32
BF16 = jnp.bfloat16
NX, NY, NZ = 4, 4, 8
BLOCK = 64
LANES = 128
SEMAPHORES = 176
BEFORE_GRAM = 4

CHUNKS = (
    ("z", 0, 32, False),
    ("y", 32, 32, False),
    ("x", 64, 32, False),
    ("z", 96, 32, False),
    ("x", 128, 32, False),
    ("y", 160, 32, True),
    ("x", 192, 32, False),
    ("z", 224, 32, False),
    ("x", 256, 32, False),
    ("y", 288, 32, True),
)

ORDER = (
    ("za", 0), ("gram_start", -1), ("ya", 1), ("xa", 2), ("za", 3), ("gram_plane", -1), ("xa", 4), ("ya", 5),
    ("xa", 6), ("zb", 0), ("yb", 1), ("za", 7), ("xb", 2), ("xa", 8), ("ya", 9), ("gram_line", -1), ("zb", 3),
    ("xb", 4), ("yb", 5), ("xb", 6), ("y2", 1), ("x2", 2), ("z2", 0), ("yb", 9), ("xb", 8), ("zb", 7),
    ("y2", 5), ("x2", 4), ("y3", 2), ("z3", 0), ("gram_spread", -1), ("x2", 6), ("y3", 1), ("y2", 9),
    ("z2", 3), ("y3", 4), ("x2", 8), ("y3", 5), ("c4", 0), ("y3", 6), ("z2", 7), ("z3", 3), ("gram_core", -1),
    ("y3", 9), ("c4", 2), ("c4", 1), ("y3", 8), ("gram_ready", -1), ("c4", 4), ("factor", 0), ("factor", 1),
    ("z3", 7), ("c5", 0), ("c4", 5), ("c4", 3), ("c4", 6), ("factor", 2), ("factor", 3), ("c4", 9), ("c5", 2),
    ("factor", 4), ("c5", 1), ("c4", 7), ("c4", 8), ("factor", 5), ("c5", 4), ("c6", 0), ("c5", 5),
    ("factor", 6), ("c5", 9), ("c5", 3), ("c5", 6), ("factor", 7), ("c6", 2), ("factor", 8), ("factor", 9),
    ("c6", 1), ("c5", 7), ("factor", 10), ("c5", 8), ("c6", 4), ("factor", 11), ("factor", 12), ("c6", 3),
    ("factor", 13), ("c6", 6), ("c6", 5), ("factor", 14), ("basis", -1), ("c6", 7), ("c6", 9), ("c6", 8),
)


def split(value):
    high = value.astype(BF16)
    return high, (value - high.astype(F32)).astype(BF16)


def eliminate(state, first, last):
    width = state.shape[1]
    row_in_group = lax.broadcasted_iota(jnp.int32, (8, width), 0)
    done = []
    for group in range(first, last):
        left = state.shape[0]
        head = state[0:8, :]
        columns = [
            jnp.broadcast_to(state[:, 8 * group + j : 8 * group + j + 1], (left, width))
            for j in range(8)
        ]
        pivot_rows, pivot_cols = [], []
        for j in range(8):
            inv = lax.rsqrt(columns[j][j : j + 1, :])
            row = head[j : j + 1, :] * inv
            col = columns[j] * inv
            pivot_rows.append(row)
            pivot_cols.append(col)
            if j < 7:
                head = head - col[0:8] * row
            for later in range(j + 1, 8):
                columns[later] = columns[later] - col * col[later : later + 1, :]
        out = jnp.broadcast_to(pivot_rows[0], (8, width))
        for j in range(1, 8):
            out = jnp.where(row_in_group == j, pivot_rows[j], out)
        done.append(out)
        if left > 8:
            state = state[8:, :]
            for j in range(8):
                state = state - pivot_cols[j][8:] * pivot_rows[j]
    return jnp.concatenate(done, axis=0), state


def factor_step(m_ref, block_ref, step, phase):
    k = m_ref.shape[0]
    lo, hi = step * BLOCK, (step + 1) * BLOCK
    half, groups = BLOCK // 2, BLOCK // 8
    rows = lax.broadcasted_iota(jnp.int32, (BLOCK, BLOCK), 0)
    cols = lax.broadcasted_iota(jnp.int32, (BLOCK, BLOCK), 1)
    identity = jnp.where(rows == cols, 1.0, 0.0).astype(F32)
    if phase == 0:
        state = jnp.concatenate([m_ref[lo:hi, lo:hi], identity], axis=1)
        block_ref[0:half, :], block_ref[half:, :] = eliminate(state, 0, groups // 2)
    elif phase == 1:
        done, _ = eliminate(block_ref[half:, :], groups // 2, groups)
        inverse = jnp.concatenate([block_ref[0:half, BLOCK:], done[:, BLOCK:]], axis=0)
        m_ref[lo:hi, lo:hi] = identity
        m_ref[lo:hi, :] = jnp.dot(
            inverse, m_ref[lo:hi, :], precision=HIGHEST, preferred_element_type=F32
        )
    elif hi < k:
        panel = m_ref[lo:hi, :]
        m_ref[hi:, lo:hi] = jnp.zeros((k - hi, BLOCK), F32)
        m_ref[hi:, :] -= lax.dot_general(
            panel[:, hi:], panel, (((0,), (0,)), ((), ())),
            precision=HIGHEST, preferred_element_type=F32,
        )


def kernel(n_total, a_hbm, om_hbm, basis_hbm, total_hbm, inv_hbm,
           a_buf, om_buf, sketch, halves, to_core, from_core, part, total,
           folded, g_core, g_plane, g_line, g_sum, mat, block, basis_t, load_sem, out_sem, sems, *flat_bufs):
    k, rows_here = sketch.shape
    bufs = [flat_bufs[4 * i : 4 * i + 4] for i in range(len(CHUNKS))]
    wide, narrow = lax.axis_index("wide"), lax.axis_index("narrow")
    x, z = lax.rem(wide, NX), wide // NX
    y, c = narrow // 2, lax.rem(narrow, 2)

    def device(xx, yy, zz, cc):
        return (zz * NX + xx, yy * 2 + cc)

    sibling = device(x, y, z, 1 - c)
    on_x = [(lax.rem(x + d, NX), device(lax.rem(x + d, NX), y, z, c)) for d in range(1, NX)]
    on_y = [(lax.rem(y + d, NY), device(x, lax.rem(y + d, NY), z, c)) for d in range(1, NY)]
    on_z = [(lax.rem(z + d, NZ), device(x, y, lax.rem(z + d, NZ), c)) for d in range(1, NZ)]
    place = y * NX + x
    on_plane = []
    for d in range(1, NX * NY):
        other = lax.rem(place + d, NX * NY)
        on_plane.append((other, device(lax.rem(other, NX), other // NX, z, c)))

    used = [0]
    pending = []

    def exchange(size_like):
        at = used[0]
        used[0] += 2
        pending.append((at, size_like))
        return at

    def send(at, src, dst, to):
        pltpu.make_async_remote_copy(
            src_ref=src, dst_ref=dst, send_sem=sems.at[at], recv_sem=sems.at[at + 1],
            device_id=to, device_id_type=MESH,
        ).start()

    def wait_bytes(sem, like):
        pltpu.make_async_copy(like, like, sem).wait()

    def received(at, like):
        wait_bytes(sems.at[at + 1], like)

    barrier = pltpu.get_barrier_semaphore()
    partners = [sibling] + [to for _, to in on_plane] + [to for _, to in on_z]
    n_blocks, _, width = a_buf.shape
    loads = []
    for j in range(n_blocks):
        loads.append((
            pltpu.make_async_copy(a_hbm.at[:, pl.ds(j * width, width)], a_buf.at[j], load_sem.at[j]),
            pltpu.make_async_copy(om_hbm.at[:, pl.ds(j * width, width)], om_buf.at[j], load_sem.at[n_blocks + j]),
        ))
    for first, second in loads:
        first.start()
        second.start()
    for to in partners:
        pl.semaphore_signal(barrier, inc=1, device_id=to, device_id_type=MESH)

    for j in range(n_blocks):
        loads[j][0].wait()
        loads[j][1].wait()
        term = lax.dot_general(
            om_buf[j], a_buf[j], (((1,), (1,)), ((), ())), preferred_element_type=F32
        )
        if j == 0:
            sketch[...] = term
        else:
            sketch[...] += term

    value = sketch[...]
    high, low = split(value)
    halves[:, 0:rows_here] = high
    halves[:, rows_here:] = low

    def project(block, dst, at, first):
        rows = pl.ds(first, k // 2)
        cols = a_buf[block]
        res = jnp.dot(
            halves[rows, :], jnp.concatenate([cols, cols], axis=0), preferred_element_type=F32
        )
        for t in range(NZ):
            dst[at, t, rows, :] = res[:, t * LANES : (t + 1) * LANES]

    def project_half(mine, first):
        for o in range(NY):
            project(2 * o + (c if mine else 1 - c), part if mine else to_core, o, first)

    ex_chunk = []

    def to_sibling(chunks):
        for _, first, n, _ in chunks:
            rows = pl.ds(first, n)
            at = exchange(from_core.at[:, :, rows, :])
            ex_chunk.append(at)
            send(at, to_core.at[:, :, rows, :], from_core.at[:, :, rows, :], sibling)

    project_half(False, 0)
    pl.semaphore_wait(barrier, len(partners))
    to_sibling(CHUNKS[:BEFORE_GRAM])
    project_half(True, 0)
    project_half(False, k // 2)

    half_rows = g_core.shape[0]
    mine = pl.multiple_of(c * half_rows, 8)
    yours = pl.multiple_of((1 - c) * half_rows, 8)

    def gram_start(ch):
        gram = lax.dot_general(
            sketch[...], sketch[...], (((1,), (1,)), ((), ())),
            precision=HIGHEST, preferred_element_type=F32,
        )
        folded[...] = jnp.zeros(folded.shape, F32)
        folded[0:128, 0:k] = gram[0:128, :]
        folded[128:256, 0 : k - 128] = gram[128:256, 128:]
        folded[128 : k - 128, 256 : k] = gram[256:, 256:]
        send(began("e", -1, g_core), folded.at[pl.ds(yours, half_rows)], g_core, sibling)
        to_sibling(CHUNKS[BEFORE_GRAM:])
        project_half(True, k // 2)

    my_tile = pl.multiple_of(c * half_rows + place * 8, 8)

    half = NZ // 2

    def rows_of(ch):
        return pl.ds(CHUNKS[ch][1], CHUNKS[ch][2])

    def quarter(ch, d):
        q = CHUNKS[ch][2] // NX
        return pl.ds(pl.multiple_of(CHUNKS[ch][1] + lax.rem(x + d, NX) * q, 8), q)

    flying = {}

    def began(name, ch, like):
        at = exchange(like)
        flying[name, ch] = (at, like)
        return at

    def arrived(name, ch):
        received(*flying[name, ch])

    def summed(buf, n):
        acc = buf[0]
        for d in range(1, n):
            acc = acc + buf[d]
        return acc

    def from_sibling(ch):
        rows = rows_of(ch)
        received(ex_chunk[ch], from_core.at[:, :, rows, :])

        def add(o, carry):
            part[o, :, rows, :] += from_core[o, :, rows, :]
            return carry

        lax.fori_loop(0, NY, add, 0)

    far, up_y, down_y = [lax.rem(y + d, NY) for d in (2, 1, 3)]

    def ya(ch):
        from_sibling(ch)
        buf, rows = bufs[ch][0], rows_of(ch)
        at = began("a", ch, buf)
        send(at, part.at[far, 0:half, rows, :], buf.at[0], on_y[0][1])
        send(at, part.at[far, half:NZ, rows, :], buf.at[1], on_y[2][1])

    def yb(ch):
        arrived("a", ch)
        old, buf, rows = bufs[ch][0], bufs[ch][1], rows_of(ch)
        part[up_y, 0:half, rows, :] += old[0]
        part[down_y, half:NZ, rows, :] += old[1]
        at = began("b", ch, buf)
        send(at, part.at[up_y, :, rows, :], buf.at[0], on_y[0][1])
        send(at, part.at[down_y, :, rows, :], buf.at[1], on_y[2][1])

    def y2(ch):
        arrived("b", ch)
        old, buf, rows = bufs[ch][1], bufs[ch][2], rows_of(ch)
        part[y, :, rows, :] += old[0] + old[1]
        at = began("2", ch, buf)
        for d in range(1, NX):
            send(at, part.at[y, :, quarter(ch, d), :], buf.at[d - 1], on_x[d - 1][1])

    def y3(ch):
        arrived("2", ch)
        old, buf, rows = bufs[ch][2], bufs[ch][3], quarter(ch, 0)
        part[y, :, rows, :] += summed(old, 3)
        at = began("3", ch, buf)
        for d, (zz, to) in enumerate(on_z):
            send(at, part.at[y, zz, rows, :], buf.at[d], to)

    def xa(ch):
        from_sibling(ch)
        buf, rows = bufs[ch][0], quarter(ch, 2)
        at = began("a", ch, buf)
        send(at, part.at[:, 0:half, rows, :], buf.at[0], on_x[0][1])
        send(at, part.at[:, half:NZ, rows, :], buf.at[1], on_x[2][1])

    def xb(ch):
        arrived("a", ch)
        old, buf = bufs[ch][0], bufs[ch][1]
        up, down = quarter(ch, 1), quarter(ch, 3)
        part[:, 0:half, up, :] += old[0]
        part[:, half:NZ, down, :] += old[1]
        at = began("b", ch, buf)
        send(at, part.at[:, :, up, :], buf.at[0], on_x[0][1])
        send(at, part.at[:, :, down, :], buf.at[1], on_x[2][1])

    def x2(ch):
        arrived("b", ch)
        old, buf, rows = bufs[ch][1], bufs[ch][2], quarter(ch, 0)
        part[:, :, rows, :] += old[0] + old[1]
        at = began("2", ch, buf)
        for d, (yy, to) in enumerate(on_y):
            send(at, part.at[yy, :, rows, :], buf.at[d], to)

    def away(d):
        return lax.rem(z + d, NZ), on_z[d - 1][1]

    def za(ch):
        from_sibling(ch)
        buf, rows = bufs[ch][0], rows_of(ch)
        at = began("a", ch, buf)
        send(at, part.at[:, away(5)[0], rows, :], buf.at[0], away(7)[1])
        send(at, part.at[:, away(3)[0], rows, :], buf.at[1], away(1)[1])
        send(at, part.at[0:2, away(4)[0], rows, :], buf.at[2, 0:2], away(2)[1])
        send(at, part.at[2:NY, away(4)[0], rows, :], buf.at[2, 2:NY], away(6)[1])

    def zb(ch):
        arrived("a", ch)
        old, buf, rows = bufs[ch][0], bufs[ch][1], rows_of(ch)
        down, up = away(6)[0], away(2)[0]
        part[:, down, rows, :] += old[0]
        part[2:NY, down, rows, :] += old[2, 2:NY]
        part[:, up, rows, :] += old[1]
        part[0:2, up, rows, :] += old[2, 0:2]
        at = began("b", ch, buf)
        for slot, d in enumerate((1, 7, 2, 6)):
            zz, to = away(d)
            send(at, part.at[:, zz, rows, :], buf.at[slot], to)

    def z2(ch):
        arrived("b", ch)
        old, buf, rows = bufs[ch][1], bufs[ch][2], rows_of(ch)
        part[:, z, rows, :] += summed(old, 4)
        at = began("2", ch, buf)
        for d, (yy, to) in enumerate(on_y):
            send(at, part.at[yy, z, rows, :], buf.at[d], to)

    def z3(ch):
        arrived("2", ch)
        old, buf, rows = bufs[ch][2], bufs[ch][3], rows_of(ch)
        part[y, z, rows, :] += summed(old, 3)
        at = began("3", ch, buf)
        for d in range(1, NX):
            send(at, part.at[y, z, quarter(ch, d), :], buf.at[d - 1], on_x[d - 1][1])

    def c4(ch):
        arrived("3", ch)
        old, rows, q = bufs[ch][3], quarter(ch, 0), CHUNKS[ch][2] // NX
        total[z, rows, :] = part[y, z, rows, :] + summed(old, old.shape[0])
        line = on_x if CHUNKS[ch][3] else on_z
        at = began("4", ch, total.at[0 : len(line), 0:q, :])
        for _, to in line:
            send(at, total.at[z, rows, :], total.at[z, rows, :], to)

    def c5(ch):
        arrived("4", ch)
        n = CHUNKS[ch][2]
        if CHUNKS[ch][3]:
            at = began("5", ch, total.at[0 : NZ - 1, 0:n, :])
            for _, to in on_z:
                send(at, total.at[z, rows_of(ch), :], total.at[z, rows_of(ch), :], to)
        else:
            at = began("5", ch, total.at[:, 0 : 3 * n // NX, :])
            for _, to in on_x:
                send(at, total.at[:, quarter(ch, 0), :], total.at[:, quarter(ch, 0), :], to)

    outs = []

    def c6(ch):
        arrived("5", ch)
        copy = pltpu.make_async_copy(
            total.at[:, rows_of(ch), :], total_hbm.at[:, rows_of(ch), :], out_sem.at[2 + ch]
        )
        copy.start()
        outs.append(copy)

    tile = pl.ds(my_tile, 8)

    def gram_plane(ch):
        arrived("e", -1)
        folded[pl.ds(mine, half_rows)] += g_core[...]
        at = began("f", -1, g_plane)
        for d, (other, to) in enumerate(on_plane):
            src = folded.at[pl.ds(pl.multiple_of(c * half_rows + other * 8, 8), 8)]
            send(at, src, g_plane.at[d], to)

    def gram_line(ch):
        arrived("f", -1)
        g_line[z] = folded[tile, :] + summed(g_plane, NX * NY - 1)
        at = began("g", -1, g_plane.at[0 : NZ - 1])
        for _, to in on_z:
            send(at, g_line.at[z], g_line.at[z], to)

    def gram_spread(ch):
        arrived("g", -1)
        g_sum[tile, :] = summed(g_line, NZ)
        at = began("h", -1, g_plane)
        for _, to in on_plane:
            send(at, g_sum.at[tile], g_sum.at[tile], to)

    def gram_core(ch):
        arrived("h", -1)
        at = began("i", -1, g_core)
        my_half = pl.ds(mine, half_rows)
        send(at, g_sum.at[my_half], g_sum.at[my_half], sibling)

    def gram_ready(ch):
        arrived("i", -1)
        mat[0:128, :] = g_sum[0:128, 0:k]
        mat[128:256, 128:] = g_sum[128:256, 0 : k - 128]
        mat[256:, 256:] = g_sum[128 : k - 128, 256 : k]

    def factor(i):
        factor_step(mat, block, i // 3, i % 3)

    def basis(ch):
        rows = lax.broadcasted_iota(jnp.int32, (k, k), 0)
        cols = lax.broadcasted_iota(jnp.int32, (k, k), 1)
        mat[...] = jnp.where(rows >= cols, mat[...], 0.0)
        basis_t[...] = jnp.dot(
            mat[...], sketch[...], precision=HIGHEST, preferred_element_type=F32
        ) * math.sqrt(n_total)
        for j, (src, dst) in enumerate(((mat, inv_hbm), (basis_t, basis_hbm))):
            copy = pltpu.make_async_copy(src, dst, out_sem.at[j])
            copy.start()
            outs.append(copy)

    steps = dict(
        ya=ya, yb=yb, y2=y2, y3=y3, xa=xa, xb=xb, x2=x2, za=za, zb=zb, z2=z2, z3=z3, c4=c4, c5=c5, c6=c6,
        gram_start=gram_start, gram_plane=gram_plane, gram_line=gram_line, gram_spread=gram_spread,
        gram_core=gram_core, gram_ready=gram_ready, factor=factor, basis=basis,
    )
    for name, arg in ORDER:
        steps[name](arg)
    for copy in outs:
        copy.wait()
    for at, like in pending:
        wait_bytes(sems.at[at], like)


def finish_kernel(n_total, basis_in, total_ref, inv_ref, basis_out, coef_ref):
    basis_out[...] = basis_in[...]
    tiles = total_ref.shape[0]
    inv_high, inv_low = split(inv_ref[...])
    high, low = split(jnp.concatenate([total_ref[t] for t in range(tiles)], axis=1))
    coef_ref[...] = jnp.dot(
        jnp.concatenate([inv_high, inv_low, inv_high], axis=1),
        jnp.concatenate([high, high, low], axis=0),
        preferred_element_type=F32,
    ) * (1.0 / math.sqrt(n_total))


def per_device(activations, test_matrix):
    rows, d = activations.shape
    k = test_matrix.shape[1]
    n_total = rows * lax.axis_size("wide") * lax.axis_size("narrow")
    width = d // (2 * NY)
    bufs = []
    half = NZ // 2
    for axis, _, n, _ in CHUNKS:
        q = n // NX
        if axis == "y":
            shapes = ((2, half, n, LANES), (2, NZ, n, LANES), (3, NZ, q, LANES), (7, q, LANES))
        elif axis == "x":
            shapes = (
                (2, NY, half, q, LANES), (2, NY, NZ, q, LANES), (3, NZ, q, LANES), (7, q, LANES)
            )
        else:
            shapes = ((3, NY, n, LANES), (4, NY, n, LANES), (3, n, LANES), (3, q, LANES))
        bufs += [pltpu.VMEM(s, F32) for s in shapes]
    block = (NY, NZ, k, LANES)
    hbm = pl.BlockSpec(memory_space=pl.ANY)
    basis_t, total, inverse = pl.pallas_call(
        functools.partial(kernel, n_total),
        out_shape=(
            jax.ShapeDtypeStruct((k, rows), F32),
            jax.ShapeDtypeStruct((NZ, k, LANES), F32),
            jax.ShapeDtypeStruct((k, k), F32),
        ),
        in_specs=[hbm] * 2,
        out_specs=(hbm, hbm, hbm),
        scratch_shapes=[
            pltpu.VMEM((d // width, rows, width), BF16),
            pltpu.VMEM((d // width, k, width), BF16),
            pltpu.VMEM((k, rows), F32),
            pltpu.VMEM((k, 2 * rows), BF16),
            pltpu.VMEM(block, F32),
            pltpu.VMEM(block, F32),
            pltpu.VMEM(block, F32),
            pltpu.VMEM((NZ, k, LANES), F32),
            pltpu.VMEM((256, 384), F32),
            pltpu.VMEM((128, 384), F32),
            pltpu.VMEM((NX * NY - 1, 8, 384), F32),
            pltpu.VMEM((NZ, 8, 384), F32),
            pltpu.VMEM((256, 384), F32),
            pltpu.VMEM((k, k), F32),
            pltpu.VMEM((BLOCK, 2 * BLOCK), F32),
            pltpu.VMEM((k, rows), F32),
            pltpu.SemaphoreType.DMA((2 * d // width,)),
            pltpu.SemaphoreType.DMA((2 + len(CHUNKS),)),
            pltpu.SemaphoreType.DMA((SEMAPHORES,)),
        ] + bufs,
        compiler_params=pltpu.CompilerParams(
            collective_id=0, has_side_effects=True, vmem_limit_bytes=56 * 1024 * 1024
        ),
        name="range_finder",
    )(activations, test_matrix.T)
    steps = 2
    by_columns = pl.BlockSpec((k, rows // steps), lambda i: (0, i))
    basis_t, coeffs = pl.pallas_call(
        functools.partial(finish_kernel, n_total),
        grid=(steps,),
        out_shape=(
            jax.ShapeDtypeStruct((k, rows), F32),
            jax.ShapeDtypeStruct((k, width), F32),
        ),
        in_specs=[
            by_columns,
            pl.BlockSpec((NZ // steps, k, LANES), lambda i: (i, 0, 0)),
            pl.BlockSpec((k, k), lambda i: (0, 0)),
        ],
        out_specs=(by_columns, pl.BlockSpec((k, width // steps), lambda i: (0, i))),
        name="apply_inverse",
    )(basis_t, total, inverse)
    return basis_t.T, coeffs


def solution(mesh):
    return jax.shard_map(
        per_device,
        mesh=mesh,
        in_specs=(P(("wide", "narrow"), None), P()),
        out_specs=(P(("wide", "narrow"), None), P(None, "narrow")),
        check_vma=False,
    )
```

```python
import functools
import math

import jax
import jax.numpy as jnp
from jax import lax
from jax.experimental import pallas as pl
from jax.experimental.pallas import tpu as pltpu
from jax.sharding import PartitionSpec as P

MESH = pl.DeviceIdType.MESH
HIGHEST = lax.Precision.HIGHEST
F32 = jnp.float32
BF16 = jnp.bfloat16
NX, NY, NZ = 4, 4, 8
BLOCK = 64
LANES = 128
SEMAPHORES = 176
LAST_STEPS = 5
BEFORE_GRAM = 4

CHUNKS = (
    ("z", 0, 32, False),
    ("y", 32, 32, False),
    ("x", 64, 32, False),
    ("z", 96, 32, False),
    ("x", 128, 32, False),
    ("y", 160, 32, True),
    ("x", 192, 32, False),
    ("z", 224, 32, False),
    ("x", 256, 32, False),
    ("y", 288, 32, True),
)

ORDER = (
    ("za", 0), ("gram_start", -1), ("ya", 1), ("xa", 2), ("za", 3), ("gram_plane", -1), ("xa", 4), ("ya", 5),
    ("xa", 6), ("zb", 0), ("yb", 1), ("za", 7), ("xb", 2), ("xa", 8), ("ya", 9), ("gram_line", -1), ("zb", 3),
    ("xb", 4), ("yb", 5), ("xb", 6), ("y2", 1), ("x2", 2), ("z2", 0), ("yb", 9), ("xb", 8), ("zb", 7),
    ("y2", 5), ("x2", 4), ("y3", 2), ("z3", 0), ("gram_spread", -1), ("x2", 6), ("y3", 1), ("y2", 9),
    ("z2", 3), ("y3", 4), ("x2", 8), ("y3", 5), ("c4", 0), ("y3", 6), ("z2", 7), ("z3", 3), ("gram_core", -1),
    ("y3", 9), ("c4", 2), ("c4", 1), ("y3", 8), ("gram_ready", -1), ("c4", 4), ("factor", 0), ("factor", 1),
    ("z3", 7), ("c5", 0), ("c4", 5), ("c4", 3), ("c4", 6), ("factor", 2), ("factor", 3), ("c4", 9), ("c5", 2),
    ("factor", 4), ("c5", 1), ("c4", 7), ("c4", 8), ("factor", 5), ("c5", 4), ("c6", 0), ("c5", 5),
    ("factor", 6), ("c5", 9), ("c5", 3), ("c5", 6), ("factor", 7), ("c6", 2), ("factor", 8), ("factor", 9),
    ("c6", 1), ("c5", 7), ("factor", 10), ("c5", 8), ("c6", 4), ("factor", 11), ("factor", 12), ("c6", 3),
    ("factor", 13), ("c6", 6), ("c6", 5), ("factor", 14), ("basis", -1), ("c6", 7), ("c6", 9), ("c6", 8),
)


def split(value):
    high = value.astype(BF16)
    return high, (value - high.astype(F32)).astype(BF16)


def eliminate(state, first, last):
    width = state.shape[1]
    row_in_group = lax.broadcasted_iota(jnp.int32, (8, width), 0)
    done = []
    for group in range(first, last):
        left = state.shape[0]
        head = state[0:8, :]
        columns = [
            jnp.broadcast_to(state[:, 8 * group + j : 8 * group + j + 1], (left, width))
            for j in range(8)
        ]
        pivot_rows, pivot_cols = [], []
        for j in range(8):
            inv = lax.rsqrt(columns[j][j : j + 1, :])
            row = head[j : j + 1, :] * inv
            col = columns[j] * inv
            pivot_rows.append(row)
            pivot_cols.append(col)
            if j < 7:
                head = head - col[0:8] * row
            for later in range(j + 1, 8):
                columns[later] = columns[later] - col * col[later : later + 1, :]
        out = jnp.broadcast_to(pivot_rows[0], (8, width))
        for j in range(1, 8):
            out = jnp.where(row_in_group == j, pivot_rows[j], out)
        done.append(out)
        if left > 8:
            state = state[8:, :]
            for j in range(8):
                state = state - pivot_cols[j][8:] * pivot_rows[j]
    return jnp.concatenate(done, axis=0), state


def factor_step(m_ref, block_ref, step, phase):
    k = m_ref.shape[0]
    lo, hi = step * BLOCK, (step + 1) * BLOCK
    half, groups = BLOCK // 2, BLOCK // 8
    rows = lax.broadcasted_iota(jnp.int32, (BLOCK, BLOCK), 0)
    cols = lax.broadcasted_iota(jnp.int32, (BLOCK, BLOCK), 1)
    identity = jnp.where(rows == cols, 1.0, 0.0).astype(F32)
    if phase == 0:
        state = jnp.concatenate([m_ref[lo:hi, lo:hi], identity], axis=1)
        block_ref[0:half, :], block_ref[half:, :] = eliminate(state, 0, groups // 2)
    elif phase == 1:
        done, _ = eliminate(block_ref[half:, :], groups // 2, groups)
        inverse = jnp.concatenate([block_ref[0:half, BLOCK:], done[:, BLOCK:]], axis=0)
        m_ref[lo:hi, lo:hi] = identity
        m_ref[lo:hi, :] = jnp.dot(
            inverse, m_ref[lo:hi, :], precision=HIGHEST, preferred_element_type=F32
        )
    elif hi < k:
        panel = m_ref[lo:hi, :]
        m_ref[hi:, lo:hi] = jnp.zeros((k - hi, BLOCK), F32)
        m_ref[hi:, :] -= lax.dot_general(
            panel[:, hi:], panel, (((0,), (0,)), ((), ())),
            precision=HIGHEST, preferred_element_type=F32,
        )


def kernel(n_total, a_hbm, om_hbm, basis_hbm, total_hbm, inv_hbm,
           a_buf, om_buf, sketch, halves, to_core, from_core, part, total,
           folded, g_core, g_plane, g_line, g_sum, mat, block, basis_t, load_sem, out_sem, sems, *flat_bufs):
    k, rows_here = sketch.shape
    bufs = [flat_bufs[4 * i : 4 * i + 4] for i in range(len(CHUNKS))]
    wide, narrow = lax.axis_index("wide"), lax.axis_index("narrow")
    x, z = lax.rem(wide, NX), wide // NX
    y, c = narrow // 2, lax.rem(narrow, 2)

    def device(xx, yy, zz, cc):
        return (zz * NX + xx, yy * 2 + cc)

    sibling = device(x, y, z, 1 - c)
    on_x = [(lax.rem(x + d, NX), device(lax.rem(x + d, NX), y, z, c)) for d in range(1, NX)]
    on_y = [(lax.rem(y + d, NY), device(x, lax.rem(y + d, NY), z, c)) for d in range(1, NY)]
    on_z = [(lax.rem(z + d, NZ), device(x, y, lax.rem(z + d, NZ), c)) for d in range(1, NZ)]
    place = y * NX + x
    on_plane = []
    for d in range(1, NX * NY):
        other = lax.rem(place + d, NX * NY)
        on_plane.append((other, device(lax.rem(other, NX), other // NX, z, c)))

    used = [0]
    pending = []
    late = []

    def exchange(size_like):
        at = used[0]
        used[0] += 2
        pending.append((at, size_like))
        return at

    def send(at, src, dst, to):
        pltpu.make_async_remote_copy(
            src_ref=src, dst_ref=dst, send_sem=sems.at[at], recv_sem=sems.at[at + 1],
            device_id=to, device_id_type=MESH,
        ).start()

    def wait_bytes(sem, like):
        pltpu.make_async_copy(like, like, sem).wait()

    def received(at, like):
        wait_bytes(sems.at[at + 1], like)

    barrier = pltpu.get_barrier_semaphore()
    partners = [sibling] + [to for _, to in on_plane] + [to for _, to in on_z]
    n_blocks, _, width = a_buf.shape
    loads = []
    for j in range(n_blocks):
        loads.append((
            pltpu.make_async_copy(a_hbm.at[:, pl.ds(j * width, width)], a_buf.at[j], load_sem.at[j]),
            pltpu.make_async_copy(om_hbm.at[:, pl.ds(j * width, width)], om_buf.at[j], load_sem.at[n_blocks + j]),
        ))
    for first, second in loads:
        first.start()
        second.start()
    for to in partners:
        pl.semaphore_signal(barrier, inc=1, device_id=to, device_id_type=MESH)

    for j in range(n_blocks):
        loads[j][0].wait()
        loads[j][1].wait()
        term = lax.dot_general(
            om_buf[j], a_buf[j], (((1,), (1,)), ((), ())), preferred_element_type=F32
        )
        if j == 0:
            sketch[...] = term
        else:
            sketch[...] += term

    value = sketch[...]
    high, low = split(value)
    halves[:, 0:rows_here] = high
    halves[:, rows_here:] = low

    def project(block, dst, at, first):
        rows = pl.ds(first, k // 2)
        cols = a_buf[block]
        res = jnp.dot(
            halves[rows, :], jnp.concatenate([cols, cols], axis=0), preferred_element_type=F32
        )
        for t in range(NZ):
            dst[at, t, rows, :] = res[:, t * LANES : (t + 1) * LANES]

    def project_half(mine, first):
        for o in range(NY):
            project(2 * o + (c if mine else 1 - c), part if mine else to_core, o, first)

    ex_chunk = []

    def to_sibling(chunks):
        for _, first, n, _ in chunks:
            rows = pl.ds(first, n)
            at = exchange(from_core.at[:, :, rows, :])
            ex_chunk.append(at)
            send(at, to_core.at[:, :, rows, :], from_core.at[:, :, rows, :], sibling)

    project_half(False, 0)
    pl.semaphore_wait(barrier, len(partners))
    to_sibling(CHUNKS[:BEFORE_GRAM])
    project_half(True, 0)
    project_half(False, k // 2)

    half_rows = g_core.shape[0]
    mine = pl.multiple_of(c * half_rows, 8)
    yours = pl.multiple_of((1 - c) * half_rows, 8)

    def gram_start(ch):
        gram = lax.dot_general(
            sketch[...], sketch[...], (((1,), (1,)), ((), ())),
            precision=HIGHEST, preferred_element_type=F32,
        )
        folded[...] = jnp.zeros(folded.shape, F32)
        folded[0:128, 0:k] = gram[0:128, :]
        folded[128:256, 0 : k - 128] = gram[128:256, 128:]
        folded[128 : k - 128, 256 : k] = gram[256:, 256:]
        send(began("e", -1, g_core), folded.at[pl.ds(yours, half_rows)], g_core, sibling)
        to_sibling(CHUNKS[BEFORE_GRAM:])
        project_half(True, k // 2)

    my_tile = pl.multiple_of(c * half_rows + place * 8, 8)

    half = NZ // 2

    def rows_of(ch):
        return pl.ds(CHUNKS[ch][1], CHUNKS[ch][2])

    def quarter(ch, d):
        q = CHUNKS[ch][2] // NX
        return pl.ds(pl.multiple_of(CHUNKS[ch][1] + lax.rem(x + d, NX) * q, 8), q)

    flying = {}

    def began(name, ch, like):
        at = exchange(like)
        if name in ("4", "5"):
            late.append(at)
        flying[name, ch] = (at, like)
        return at

    def arrived(name, ch):
        received(*flying[name, ch])

    def summed(buf, n):
        acc = buf[0]
        for d in range(1, n):
            acc = acc + buf[d]
        return acc

    def from_sibling(ch):
        rows = rows_of(ch)
        received(ex_chunk[ch], from_core.at[:, :, rows, :])

        def add(o, carry):
            part[o, :, rows, :] += from_core[o, :, rows, :]
            return carry

        lax.fori_loop(0, NY, add, 0)

    far, up_y, down_y = [lax.rem(y + d, NY) for d in (2, 1, 3)]

    def ya(ch):
        from_sibling(ch)
        buf, rows = bufs[ch][0], rows_of(ch)
        at = began("a", ch, buf)
        send(at, part.at[far, 0:half, rows, :], buf.at[0], on_y[0][1])
        send(at, part.at[far, half:NZ, rows, :], buf.at[1], on_y[2][1])

    def yb(ch):
        arrived("a", ch)
        old, buf, rows = bufs[ch][0], bufs[ch][1], rows_of(ch)
        part[up_y, 0:half, rows, :] += old[0]
        part[down_y, half:NZ, rows, :] += old[1]
        at = began("b", ch, buf)
        send(at, part.at[up_y, :, rows, :], buf.at[0], on_y[0][1])
        send(at, part.at[down_y, :, rows, :], buf.at[1], on_y[2][1])

    def y2(ch):
        arrived("b", ch)
        old, buf, rows = bufs[ch][1], bufs[ch][2], rows_of(ch)
        part[y, :, rows, :] += old[0] + old[1]
        at = began("2", ch, buf)
        for d in range(1, NX):
            send(at, part.at[y, :, quarter(ch, d), :], buf.at[d - 1], on_x[d - 1][1])

    def y3(ch):
        arrived("2", ch)
        old, buf, rows = bufs[ch][2], bufs[ch][3], quarter(ch, 0)
        part[y, :, rows, :] += summed(old, 3)
        at = began("3", ch, buf)
        for d, (zz, to) in enumerate(on_z):
            send(at, part.at[y, zz, rows, :], buf.at[d], to)

    def xa(ch):
        from_sibling(ch)
        buf, rows = bufs[ch][0], quarter(ch, 2)
        at = began("a", ch, buf)
        send(at, part.at[:, 0:half, rows, :], buf.at[0], on_x[0][1])
        send(at, part.at[:, half:NZ, rows, :], buf.at[1], on_x[2][1])

    def xb(ch):
        arrived("a", ch)
        old, buf = bufs[ch][0], bufs[ch][1]
        up, down = quarter(ch, 1), quarter(ch, 3)
        part[:, 0:half, up, :] += old[0]
        part[:, half:NZ, down, :] += old[1]
        at = began("b", ch, buf)
        send(at, part.at[:, :, up, :], buf.at[0], on_x[0][1])
        send(at, part.at[:, :, down, :], buf.at[1], on_x[2][1])

    def x2(ch):
        arrived("b", ch)
        old, buf, rows = bufs[ch][1], bufs[ch][2], quarter(ch, 0)
        part[:, :, rows, :] += old[0] + old[1]
        at = began("2", ch, buf)
        for d, (yy, to) in enumerate(on_y):
            send(at, part.at[yy, :, rows, :], buf.at[d], to)

    def away(d):
        return lax.rem(z + d, NZ), on_z[d - 1][1]

    def za(ch):
        from_sibling(ch)
        buf, rows = bufs[ch][0], rows_of(ch)
        at = began("a", ch, buf)
        send(at, part.at[:, away(5)[0], rows, :], buf.at[0], away(7)[1])
        send(at, part.at[:, away(3)[0], rows, :], buf.at[1], away(1)[1])
        send(at, part.at[0:2, away(4)[0], rows, :], buf.at[2, 0:2], away(2)[1])
        send(at, part.at[2:NY, away(4)[0], rows, :], buf.at[2, 2:NY], away(6)[1])

    def zb(ch):
        arrived("a", ch)
        old, buf, rows = bufs[ch][0], bufs[ch][1], rows_of(ch)
        down, up = away(6)[0], away(2)[0]
        part[:, down, rows, :] += old[0]
        part[2:NY, down, rows, :] += old[2, 2:NY]
        part[:, up, rows, :] += old[1]
        part[0:2, up, rows, :] += old[2, 0:2]
        at = began("b", ch, buf)
        for slot, d in enumerate((1, 7, 2, 6)):
            zz, to = away(d)
            send(at, part.at[:, zz, rows, :], buf.at[slot], to)

    def z2(ch):
        arrived("b", ch)
        old, buf, rows = bufs[ch][1], bufs[ch][2], rows_of(ch)
        part[:, z, rows, :] += summed(old, 4)
        at = began("2", ch, buf)
        for d, (yy, to) in enumerate(on_y):
            send(at, part.at[yy, z, rows, :], buf.at[d], to)

    def z3(ch):
        arrived("2", ch)
        old, buf, rows = bufs[ch][2], bufs[ch][3], rows_of(ch)
        part[y, z, rows, :] += summed(old, 3)
        at = began("3", ch, buf)
        for d in range(1, NX):
            send(at, part.at[y, z, quarter(ch, d), :], buf.at[d - 1], on_x[d - 1][1])

    def c4(ch):
        arrived("3", ch)
        old, rows, q = bufs[ch][3], quarter(ch, 0), CHUNKS[ch][2] // NX
        total[z, rows, :] = part[y, z, rows, :] + summed(old, old.shape[0])
        line = on_x if CHUNKS[ch][3] else on_z
        at = began("4", ch, total.at[0 : len(line), 0:q, :])
        for _, to in line:
            send(at, total.at[z, rows, :], total.at[z, rows, :], to)

    def c5(ch):
        arrived("4", ch)
        n = CHUNKS[ch][2]
        if CHUNKS[ch][3]:
            at = began("5", ch, total.at[0 : NZ - 1, 0:n, :])
            for _, to in on_z:
                send(at, total.at[z, rows_of(ch), :], total.at[z, rows_of(ch), :], to)
        else:
            at = began("5", ch, total.at[:, 0 : 3 * n // NX, :])
            for _, to in on_x:
                send(at, total.at[:, quarter(ch, 0), :], total.at[:, quarter(ch, 0), :], to)

    outs = []

    def c6(ch):
        arrived("5", ch)
        copy = pltpu.make_async_copy(
            total.at[:, rows_of(ch), :], total_hbm.at[:, rows_of(ch), :], out_sem.at[2 + ch]
        )
        copy.start()
        outs.append(copy)

    tile = pl.ds(my_tile, 8)

    def gram_plane(ch):
        arrived("e", -1)
        folded[pl.ds(mine, half_rows)] += g_core[...]
        at = began("f", -1, g_plane)
        for d, (other, to) in enumerate(on_plane):
            src = folded.at[pl.ds(pl.multiple_of(c * half_rows + other * 8, 8), 8)]
            send(at, src, g_plane.at[d], to)

    def gram_line(ch):
        arrived("f", -1)
        g_line[z] = folded[tile, :] + summed(g_plane, NX * NY - 1)
        at = began("g", -1, g_plane.at[0 : NZ - 1])
        for _, to in on_z:
            send(at, g_line.at[z], g_line.at[z], to)

    def gram_spread(ch):
        arrived("g", -1)
        g_sum[tile, :] = summed(g_line, NZ)
        at = began("h", -1, g_plane)
        for _, to in on_plane:
            send(at, g_sum.at[tile], g_sum.at[tile], to)

    def gram_core(ch):
        arrived("h", -1)
        at = began("i", -1, g_core)
        my_half = pl.ds(mine, half_rows)
        send(at, g_sum.at[my_half], g_sum.at[my_half], sibling)

    def gram_ready(ch):
        arrived("i", -1)
        mat[0:128, :] = g_sum[0:128, 0:k]
        mat[128:256, 128:] = g_sum[128:256, 0 : k - 128]
        mat[256:, 256:] = g_sum[128 : k - 128, 256 : k]

    def factor(i):
        factor_step(mat, block, i // 3, i % 3)

    def basis(ch):
        rows = lax.broadcasted_iota(jnp.int32, (k, k), 0)
        cols = lax.broadcasted_iota(jnp.int32, (k, k), 1)
        mat[...] = jnp.where(rows >= cols, mat[...], 0.0)
        basis_t[...] = jnp.dot(
            mat[...], sketch[...], precision=HIGHEST, preferred_element_type=F32
        ) * math.sqrt(n_total)
        for j, (src, dst) in enumerate(((mat, inv_hbm), (basis_t, basis_hbm))):
            copy = pltpu.make_async_copy(src, dst, out_sem.at[j])
            copy.start()
            outs.append(copy)

    steps = dict(
        ya=ya, yb=yb, y2=y2, y3=y3, xa=xa, xb=xb, x2=x2, za=za, zb=zb, z2=z2, z3=z3, c4=c4, c5=c5, c6=c6,
        gram_start=gram_start, gram_plane=gram_plane, gram_line=gram_line, gram_spread=gram_spread,
        gram_core=gram_core, gram_ready=gram_ready, factor=factor, basis=basis,
    )
    for at_step, (name, arg) in enumerate(ORDER):
        if at_step == len(ORDER) - LAST_STEPS:
            early = [p for p in pending if p[0] not in late]
            for at, like in early:
                wait_bytes(sems.at[at], like)
            pending[:] = [p for p in pending if p[0] in late]
        steps[name](arg)
    for copy in outs:
        copy.wait()
    for at, like in pending:
        wait_bytes(sems.at[at], like)


def finish_kernel(n_total, basis_in, total_ref, inv_ref, basis_out, coef_ref):
    basis_out[...] = basis_in[...]
    tiles = total_ref.shape[0]
    inv_high, inv_low = split(inv_ref[...])
    high, low = split(jnp.concatenate([total_ref[t] for t in range(tiles)], axis=1))
    coef_ref[...] = jnp.dot(
        jnp.concatenate([inv_high, inv_low, inv_high], axis=1),
        jnp.concatenate([high, high, low], axis=0),
        preferred_element_type=F32,
    ) * (1.0 / math.sqrt(n_total))


def per_device(activations, test_matrix):
    rows, d = activations.shape
    k = test_matrix.shape[1]
    n_total = rows * lax.axis_size("wide") * lax.axis_size("narrow")
    width = d // (2 * NY)
    bufs = []
    half = NZ // 2
    for axis, _, n, _ in CHUNKS:
        q = n // NX
        if axis == "y":
            shapes = ((2, half, n, LANES), (2, NZ, n, LANES), (3, NZ, q, LANES), (7, q, LANES))
        elif axis == "x":
            shapes = (
                (2, NY, half, q, LANES), (2, NY, NZ, q, LANES), (3, NZ, q, LANES), (7, q, LANES)
            )
        else:
            shapes = ((3, NY, n, LANES), (4, NY, n, LANES), (3, n, LANES), (3, q, LANES))
        bufs += [pltpu.VMEM(s, F32) for s in shapes]
    block = (NY, NZ, k, LANES)
    hbm = pl.BlockSpec(memory_space=pl.ANY)
    basis_t, total, inverse = pl.pallas_call(
        functools.partial(kernel, n_total),
        out_shape=(
            jax.ShapeDtypeStruct((k, rows), F32),
            jax.ShapeDtypeStruct((NZ, k, LANES), F32),
            jax.ShapeDtypeStruct((k, k), F32),
        ),
        in_specs=[hbm] * 2,
        out_specs=(hbm, hbm, hbm),
        scratch_shapes=[
            pltpu.VMEM((d // width, rows, width), BF16),
            pltpu.VMEM((d // width, k, width), BF16),
            pltpu.VMEM((k, rows), F32),
            pltpu.VMEM((k, 2 * rows), BF16),
            pltpu.VMEM(block, F32),
            pltpu.VMEM(block, F32),
            pltpu.VMEM(block, F32),
            pltpu.VMEM((NZ, k, LANES), F32),
            pltpu.VMEM((256, 384), F32),
            pltpu.VMEM((128, 384), F32),
            pltpu.VMEM((NX * NY - 1, 8, 384), F32),
            pltpu.VMEM((NZ, 8, 384), F32),
            pltpu.VMEM((256, 384), F32),
            pltpu.VMEM((k, k), F32),
            pltpu.VMEM((BLOCK, 2 * BLOCK), F32),
            pltpu.VMEM((k, rows), F32),
            pltpu.SemaphoreType.DMA((2 * d // width,)),
            pltpu.SemaphoreType.DMA((2 + len(CHUNKS),)),
            pltpu.SemaphoreType.DMA((SEMAPHORES,)),
        ] + bufs,
        compiler_params=pltpu.CompilerParams(
            collective_id=0, has_side_effects=True, vmem_limit_bytes=56 * 1024 * 1024
        ),
        name="range_finder",
    )(activations, test_matrix.T)
    steps = 2
    by_columns = pl.BlockSpec((k, rows // steps), lambda i: (0, i))
    basis_t, coeffs = pl.pallas_call(
        functools.partial(finish_kernel, n_total),
        grid=(steps,),
        out_shape=(
            jax.ShapeDtypeStruct((k, rows), F32),
            jax.ShapeDtypeStruct((k, width), F32),
        ),
        in_specs=[
            by_columns,
            pl.BlockSpec((NZ // steps, k, LANES), lambda i: (i, 0, 0)),
            pl.BlockSpec((k, k), lambda i: (0, 0)),
        ],
        out_specs=(by_columns, pl.BlockSpec((k, width // steps), lambda i: (0, i))),
        name="apply_inverse",
    )(basis_t, total, inverse)
    return basis_t.T, coeffs


def solution(mesh):
    return jax.shard_map(
        per_device,
        mesh=mesh,
        in_specs=(P(("wide", "narrow"), None), P()),
        out_specs=(P(("wide", "narrow"), None), P(None, "narrow")),
        check_vma=False,
    )
```
